32 devices in a mesh: dp: 2 (over x), ctx: 4 (over y, core), exp: 4 (over z).
Axes of the slice: x: 2, y: 2, z: 4, core: 2. Of those that a mesh axis runs over, the one named last changes fastest.
Arguments:
- queries: bfloat16 [2, 1024, 3584], P('dp', 'ctx'), may hold values from -20 to 20
- keys: bfloat16 [2, 1024, 512], P('dp', 'ctx'), may hold values from -20 to 20
- values: bfloat16 [2, 1024, 512], P('dp', 'ctx'), may hold values from -6 to 6
- residual: bfloat16 [2, 1024, 3584], P('dp', 'ctx'), may hold values from -4 to 4
- labels: int32 [2, 8], P('dp'), may hold values from 0 to 1, as said below
- block_mask: int32 [2, 8, 8], P('dp'), may hold values from 0 to 1, as said below
- gains: float32 [2, 3584], replicated, may hold values from 0.5 to 1.5
- w_gate: bfloat16 [3584, 1216], P(None, 'exp'), may hold values from -0.09375 to 0.09375
- w_up: bfloat16 [3584, 1216], P(None, 'exp'), may hold values from -0.09375 to 0.09375
- w_down: bfloat16 [1216, 3584], P('exp'), may hold values from -0.625 to 0.625
Outputs:
- layer_out: bfloat16 [2, 1024, 3584], P('dp', ('ctx', 'exp'))
The draws below stay inside these ranges and needn't reach their ends.
Inputs may be any that keep to these rules, and one draw needn't show every extreme that they name: `labels`: per sequence a share of visual blocks is drawn, then each block's label independently. Each sequence is packed with documents made of whole blocks, the first starting at block 0. block_mask[i, j] is 1 exactly when blocks i and j lie in the same document and (j <= i, or blocks i and j are both visual with no text block between them); the diagonal is always 1.
All inputs are finite; a program needn't handle non-finite values.
Results may differ from the reference program's by a relative error of at most 0.0069.
Values may be sent and summed in bfloat16 or wider, within the bound.
No kernel may reach another device: no remote copies, remote signals or barrier semaphores. Data moves between devices by JAX's collectives and lax.ppermute only.
A program may use at most 64 MiB of HBM per device.

```python
import jax
import jax.numpy as jnp
from jax import lax

D = 3584
HEADS = 28
KV_HEADS = 4
HEAD_DIM = 128
BLOCK = 128
LEN = 1024
NBLK = 8
FFW = 608
N_DP = 2


def block_layout(key):
    first, second = jax.random.split(jax.random.fold_in(key, 11))
    third = jax.random.fold_in(key, 23)
    share = jax.random.randint(first, (N_DP, 1), 20, 81)
    rolls = jax.random.randint(second, (N_DP, NBLK), 0, 100)
    labels = (rolls < share).astype(jnp.int32)
    order = jnp.arange(NBLK, dtype=jnp.int32)
    starts = (jax.random.randint(third, (N_DP, NBLK), 0, 4) == 0).astype(jnp.int32)
    starts = jnp.where(order[None, :] == 0, 0, starts)
    documents = jnp.cumsum(starts, axis=1)
    same_doc = documents[:, :, None] == documents[:, None, :]
    runs = jnp.cumsum(1 - labels, axis=1)
    causal = order[None, :, None] >= order[None, None, :]
    joined = (labels[:, :, None] == 1) & (labels[:, None, :] == 1) & (runs[:, :, None] == runs[:, None, :])
    return (labels, ((causal | joined) & same_doc).astype(jnp.int32))


def draw_labels(key, part):
    return block_layout(key)[0]


def draw_block_mask(key, part):
    return block_layout(key)[1]


def query_key_pair(key):
    kq, kk = jax.random.split(jax.random.fold_in(key, 7), 2)
    kv_width = KV_HEADS * HEAD_DIM
    queries = jnp.clip(jax.random.normal(kq, (N_DP, LEN, D), jnp.float32), -6.0, 6.0)
    keys = jnp.clip(jax.random.normal(kk, (N_DP, LEN, kv_width), jnp.float32), -6.0, 6.0)
    return (queries, keys)


def draw_queries(key, part):
    return query_key_pair(key)[0].astype(jnp.bfloat16)


def draw_keys(key, part):
    return query_key_pair(key)[1].astype(jnp.bfloat16)


def steps_of(key, shape, cuts, smallest, top_value):
    gain, own = 1.0, jax.random.fold_in(key, 6)
    for dim, shards_of in cuts:
        draws = jnp.exp(jax.random.uniform(jax.random.fold_in(own, dim), (shards_of,), jnp.float32, smallest / len(cuts), top_value / len(cuts)))
        gain = gain * jnp.repeat(draws, shape[dim] // shards_of).reshape([-1 if axis == dim else 1 for axis in range(len(shape))])
    return gain


def centred(stream_key, shape, deviation, reach, cuts=(), kind=jnp.bfloat16):
    result = deviation * jax.random.normal(stream_key, shape, jnp.float32)
    if cuts:
        result = result * steps_of(stream_key, shape, cuts, -0.22, 0.18)
    return jnp.clip(result, -reach, reach).astype(kind)


def setup_inputs(seed: int = 0) -> dict:
    splits = jax.random.split(jax.random.key(seed), 11)
    queries = draw_queries(jax.random.fold_in(splits[10], 71), 0)
    keys = draw_keys(jax.random.fold_in(splits[10], 71), 0)
    values = centred(splits[2], (N_DP, LEN, KV_HEADS * HEAD_DIM), 1.0, 6.0, ((0, 2), (1, 4)))
    residual = centred(splits[3], (N_DP, LEN, D), 0.5, 4.0, ((0, 2), (1, 4)))
    labels = draw_labels(jax.random.fold_in(splits[10], 71), 0)
    block_mask = draw_block_mask(jax.random.fold_in(splits[10], 71), 0)
    gains = jnp.clip(1.0 + 0.1 * jax.random.normal(splits[6], (2, D), jnp.float32), 0.5, 1.5)
    w_gate = centred(splits[7], (D, 2 * FFW), D ** -0.5, 0.09375, ((1, 4),))
    w_up = centred(splits[8], (D, 2 * FFW), D ** -0.5, 0.09375, ((1, 4),))
    w_down = centred(splits[9], (2 * FFW, D), (FFW // 8) ** -0.5, 0.625, ((0, 4),))
    return {"queries": queries, "keys": keys, "values": values, "residual": residual, "labels": labels, "block_mask": block_mask, "gains": gains, "w_gate": w_gate, "w_up": w_up, "w_down": w_down}


def one_sequence(queries, keys, values, residual, labels, block_mask, gains, w_gate, w_up, w_down):
    group = HEADS // KV_HEADS
    width = FFW
    positions = jnp.arange(LEN, dtype=jnp.int32)
    blocks = positions // BLOCK
    token_label = labels[blocks]
    allowed = block_mask[blocks][:, blocks] == 1
    same = blocks[:, None] == blocks[None, :]
    causal = positions[None, :] <= positions[:, None]
    visual = token_label == 1
    allowed = allowed & (jnp.logical_not(same) | causal | visual[:, None])
    q_heads = queries.astype(jnp.float32).reshape(LEN, KV_HEADS, group, HEAD_DIM)
    k_heads = keys.astype(jnp.float32).reshape(LEN, KV_HEADS, HEAD_DIM)
    v_heads = values.astype(jnp.float32).reshape(LEN, KV_HEADS, HEAD_DIM)
    scores = jnp.einsum('qgrd,kgd->grqk', q_heads, k_heads) / jnp.sqrt(jnp.float32(HEAD_DIM))
    scores = jnp.where(allowed[None, None], scores, -jnp.inf)
    top = lax.optimization_barrier(jnp.max(scores, axis=-1, keepdims=True))
    weights = jnp.where(allowed[None, None], jnp.exp(scores - top), 0.0)
    total = lax.optimization_barrier(jnp.sum(weights, axis=-1))
    soft = weights.astype(jnp.bfloat16).astype(jnp.float32)
    mixed = jnp.einsum('grqk,kgd->qgrd', soft, v_heads)
    mixed = mixed / jnp.transpose(total, (2, 0, 1))[..., None]
    attention = mixed.reshape(LEN, D).astype(jnp.bfloat16)
    mid = residual.astype(jnp.float32) + attention.astype(jnp.float32)
    gain_rows = jnp.where(visual[:, None], gains[1][None, :], gains[0][None, :])
    normed = (mid * lax.rsqrt(lax.optimization_barrier(jnp.mean(mid * mid, axis=-1, keepdims=True)) + 1e-05) * gain_rows).astype(jnp.bfloat16)
    branch = jnp.zeros((LEN, D), jnp.float32)
    for modality in range(2):
        gate = jnp.dot(normed, w_gate[:, modality * width:(modality + 1) * width], preferred_element_type=jnp.float32)
        upper = jnp.dot(normed, w_up[:, modality * width:(modality + 1) * width], preferred_element_type=jnp.float32)
        hidden = (jax.nn.silu(gate) * upper).astype(jnp.bfloat16)
        part = jnp.dot(hidden, w_down[modality * width:(modality + 1) * width], preferred_element_type=jnp.float32)
        branch = branch + jnp.where((token_label == modality)[:, None], part, 0.0)
    return (mid + branch).astype(jnp.bfloat16)

def reference(queries, keys, values, residual, labels, block_mask, gains, w_gate, w_up, w_down):

    def single(index):
        return one_sequence(queries[index], keys[index], values[index], residual[index], labels[index], block_mask[index], gains, w_gate, w_up, w_down)
    return lax.map(single, jnp.arange(N_DP, dtype=jnp.int32))
```

```python
import functools

import jax
import jax.numpy as jnp
from jax import lax
from jax.experimental import pallas as pl
from jax.experimental.pallas import tpu as pltpu
from jax.sharding import PartitionSpec as P

KV_HEADS = 4
HEAD_DIM = 128
BLOCK = 128
LANES = 128
MASKED = -1e30
EXP2_SCALE = 1.4426950408889634 / (HEAD_DIM**0.5)
BF16 = jnp.bfloat16
F32 = jnp.float32
OVER_LAST = (((1,), (1,)), ((), ()))
LEAVE, STAY, WHOLE = range(3)
CUTS = 2
WIDE = 128


def fill_bias(bias_ref, mask_ref, labels_ref, here, shards):
    key_in = lax.broadcasted_iota(jnp.int32, (BLOCK, BLOCK), 0)
    query_in = lax.broadcasted_iota(jnp.int32, (BLOCK, BLOCK), 1)
    later = (key_in > query_in).astype(jnp.int32)
    piece_blocks = bias_ref.shape[1] // BLOCK
    any_open = jnp.int32(0)
    for c, shard_of in enumerate(shards):
        for b in range(piece_blocks):
            other = shard_of * piece_blocks + b
            is_open = mask_ref[0, here, other]
            any_open = any_open | is_open
            closed = jnp.where(other == here, 1 - labels_ref[0, here], 0) * later
            closed = jnp.where(is_open == 1, closed, 1)
            bias_ref[c, b * BLOCK : (b + 1) * BLOCK, :] = jnp.where(closed == 1, MASKED, 0.0).astype(BF16)
    return any_open


def attend(q_ref, key_refs, value_refs, bias_ref, s_buf, prior, finish):
    tile, width = q_ref.shape
    group = width // (KV_HEADS * HEAD_DIM)
    rows = group * tile
    row_ids = lax.broadcasted_iota(jnp.int32, (tile, BLOCK), 0)
    col_ids = lax.broadcasted_iota(jnp.int32, (tile, BLOCK), 1)
    picks = jnp.where(row_ids == col_ids, 1.0, 0.0).astype(BF16)
    ones = jnp.ones((key_refs[0].shape[0], HEAD_DIM), BF16)
    limits = {}

    def score(g):
        q_all = jnp.concatenate(
            [
                jnp.concatenate([q_ref[:, (g * group + h) * HEAD_DIM : (g * group + h + 1) * HEAD_DIM], picks], axis=1)
                for h in range(group)
            ],
            axis=0,
        )
        lanes = slice(g * HEAD_DIM, (g + 1) * HEAD_DIM)
        k_all = jnp.concatenate(
            [jnp.concatenate([ref[:, lanes], bias_ref[c]], axis=1) for c, ref in enumerate(key_refs)], axis=0
        )
        s = lax.dot_general(q_all, k_all, OVER_LAST, preferred_element_type=F32)
        s_buf[g % 2] = s
        top = functools.reduce(jnp.maximum, [s[:, n : n + LANES] for n in range(0, s.shape[1], LANES)])
        top = jnp.broadcast_to(jnp.max(top, axis=1, keepdims=True), (rows, LANES))
        if prior is not None:
            top = jnp.maximum(top, prior(g)[2])
        limits[g] = top

    def mix(g):
        lanes = slice(g * HEAD_DIM, (g + 1) * HEAD_DIM)
        shift = limits[g] * EXP2_SCALE
        soft = jnp.concatenate(
            [
                jnp.exp2(s_buf[g % 2, :, n : n + LANES] * EXP2_SCALE - shift).astype(BF16)
                for n in range(0, s_buf.shape[2], LANES)
            ],
            axis=1,
        )
        v_all = jnp.concatenate([jnp.concatenate([ref[:, lanes], ones], axis=1) for ref in value_refs], axis=0)
        mixed = jnp.dot(soft, v_all, preferred_element_type=F32)
        sums, totals = mixed[:, :HEAD_DIM], mixed[:, HEAD_DIM:]
        if prior is not None:
            before = prior(g)
            factor = jnp.exp2((before[2] - limits[g]) * EXP2_SCALE)
            sums = sums + before[0] * factor
            totals = totals + before[1] * factor
        finish(g, sums, totals, limits[g])

    score(0)
    for g in range(KV_HEADS):
        if g + 1 < KV_HEADS:
            score(g + 1)
        mix(g)


def near_kernel(labels_ref, mask_ref, place_ref, q_hbm, *rest):
    pieces = (len(rest) - 7) // 2
    key_refs, value_refs = rest[:pieces], rest[pieces : 2 * pieces]
    sums_ref, totals_ref, limits_ref, q_ref, bias_buf, s_buf, sem = rest[2 * pieces :]
    blocks, tile, _ = q_ref.shape
    ctx_here, section = place_ref[0], place_ref[1]

    loads = [pltpu.make_async_copy(q_hbm.at[pl.ds(t * tile, tile)], q_ref.at[t], sem.at[t]) for t in range(blocks)]
    for copy in loads:
        copy.start()
    for t in range(blocks):
        fill_bias(bias_buf.at[t], mask_ref, labels_ref, ctx_here * blocks + t, [ctx_here ^ c for c in range(pieces)])
    for copy in loads:
        copy.wait()

    def block_of(t, carry):
        @pl.when(labels_ref[0, ctx_here * blocks + t] == section)
        def _():
            def finish(g, sums, totals, limit):
                sums_ref[t, g] = sums
                totals_ref[t, g] = totals
                limits_ref[t, g] = limit

            attend(q_ref.at[t], key_refs, value_refs, bias_buf.at[t], s_buf, None, finish)

        return carry

    lax.fori_loop(0, blocks, block_of, 0)


def far_kernel(
    mode, first_piece, waited, labels_ref, mask_ref, place_ref, q_ref, res_hbm, gains_ref, sums_ref, totals_ref,
    limits_ref, *rest,
):
    rest = rest[waited:]
    outs = {LEAVE: 2 * CUTS, STAY: 2, WHOLE: 1}[mode]
    pieces = (len(rest) - outs - 13) // 2
    key_refs, value_refs = rest[:pieces], rest[pieces : 2 * pieces]
    wg_hbm, wu_hbm, wd_hbm = rest[2 * pieces : 2 * pieces + 3]
    out_refs = rest[2 * pieces + 3 : 2 * pieces + 3 + outs]
    res_buf, w_buf, wd_buf, bias_buf, s_buf, att_buf, norm_buf, hid_buf, sem, w_sem = rest[2 * pieces + 3 + outs :]
    blocks, tile, width = q_ref.shape
    units = wg_hbm.shape[0]
    up_at = w_buf.shape[0] - units
    group = width // (KV_HEADS * HEAD_DIM)
    ctx_here, section, low, first = place_ref[0], place_ref[1], place_ref[2], place_ref[4]
    chosen = {LEAVE: [1 - section], STAY: [section], WHOLE: list(range(blocks))}[mode]

    loads = []
    for i, t in enumerate(chosen):
        rows = pl.ds(pl.multiple_of(t * tile, tile), tile)
        loads.append(pltpu.make_async_copy(res_hbm.at[rows], res_buf.at[pl.ds(i * tile, tile)], sem.at[i]))
    loads.append(pltpu.make_async_copy(wg_hbm, w_buf.at[pl.ds(0, units)], w_sem.at[0]))
    loads.append(pltpu.make_async_copy(wu_hbm, w_buf.at[pl.ds(up_at, units)], w_sem.at[1]))
    later = pltpu.make_async_copy(wd_hbm, wd_buf, w_sem.at[2])
    for copy in loads:
        copy.start()
    later.start()

    matches = [labels_ref[0, ctx_here * blocks + t] == section for t in chosen]
    for i, t in enumerate(chosen):
        opened = fill_bias(
            bias_buf, mask_ref, labels_ref, ctx_here * blocks + t,
            [ctx_here ^ (first_piece + c) for c in range(pieces)],
        )

        def finish(g, sums, totals, _):
            attended = (sums / totals).astype(BF16)
            for h in range(group):
                at = (g * group + h) * HEAD_DIM
                att_buf[i * tile : (i + 1) * tile, at : at + HEAD_DIM] = attended[h * tile : (h + 1) * tile]

        def prior(g):
            return sums_ref[t, g], totals_ref[t, g], limits_ref[t, g]

        @pl.when(matches[i] & (opened > 0))
        def _():
            attend(q_ref.at[t], key_refs, value_refs, bias_buf, s_buf, prior, finish)

        @pl.when(matches[i] & (opened == 0))
        def _():
            for g in range(KV_HEADS):
                finish(g, sums_ref[t, g], totals_ref[t, g], None)

        @pl.when(jnp.logical_not(matches[i]))
        def _():
            norm_buf[i * tile : (i + 1) * tile, :] = jnp.zeros((tile, width), BF16)

    for copy in loads:
        copy.wait()

    step = 16
    for i in range(len(chosen)):

        @pl.when(matches[i])
        def _():
            gain = gains_ref[pl.ds(section, 1), :]

            def norm_rows(j, carry):
                rows = pl.ds(pl.multiple_of(i * tile + j * step, step), step)
                mid = res_buf[rows, :].astype(F32) + att_buf[rows, :].astype(F32)
                factor = lax.rsqrt(jnp.mean(mid * mid, axis=-1, keepdims=True) + 1e-05)
                norm_buf[rows, :] = (mid * factor * gain).astype(BF16)
                return carry

            lax.fori_loop(0, tile // step, norm_rows, 0)

    later.wait()
    half = tile // 2
    own = pl.ds(pl.multiple_of(low * half, half), half)
    other = pl.ds(pl.multiple_of(half - low * half, half), half)

    def mid_of(rows, cols):
        return res_buf[rows, cols].astype(F32) + att_buf[rows, cols].astype(F32)

    @pl.when(functools.reduce(jnp.logical_or, matches))
    def _():
        both = lax.dot_general(norm_buf[...], w_buf[...], OVER_LAST, preferred_element_type=F32)
        gate, upper = both[:, :units], both[:, up_at : up_at + units]
        hid_buf[...] = (gate * upper / (1.0 + jnp.exp(-gate))).astype(BF16)
        if mode == LEAVE:
            left = jnp.concatenate([hid_buf[own, :], hid_buf[other, :]], axis=0)
        elif mode == STAY:
            left = hid_buf[own, :]
            out_refs[1][...] = hid_buf[other, :]
        else:
            left = hid_buf[...]
        cut = width // CUTS
        for n in range(0, width, WIDE):
            cols = slice(n, n + WIDE)
            terms = jnp.dot(left, wd_buf[:, cols], preferred_element_type=F32)
            if mode == LEAVE:
                at = slice(n % cut, n % cut + WIDE)
                out_refs[n // cut][:, at] = terms[:half] + mid_of(own, cols)
                out_refs[CUTS + n // cut][:, at] = terms[half:].astype(BF16)
            elif mode == STAY:
                out_refs[0][:, cols] = terms + mid_of(own, cols)
            else:
                for i in range(len(chosen)):
                    span = slice(i * tile, (i + 1) * tile)
                    kept = terms[span] + mid_of(span, cols) * first.astype(F32)
                    out_refs[0][span, cols] = jnp.where(matches[i], kept, 0.0)

    @pl.when(jnp.logical_not(functools.reduce(jnp.logical_or, matches)))
    def _():
        for ref in out_refs:
            ref[...] = jnp.zeros(ref.shape, ref.dtype)


def down_kernel(labels_ref, place_ref, in_ref, base_ref, *rest):
    quarter_refs, out_ref = rest[:-1], rest[-1]
    cut = quarter_refs[0].shape[1]
    ctx_here, section, core, row = place_ref[0], place_ref[1], place_ref[3], place_ref[5]
    match = labels_ref[0, ctx_here * 2 + section] == section
    here = 2 * row + core

    @pl.when(match)
    def _():
        for i, ref in enumerate(quarter_refs):
            for n in range(0, cut, LANES):
                wide = min(WIDE, cut - n)
                if n % WIDE:
                    continue
                cols = pl.ds(pl.multiple_of((here ^ i) * cut + n, LANES), wide)
                terms = jnp.dot(in_ref[...], ref[:, n : n + wide], preferred_element_type=F32)
                out_ref[:, cols] = terms + base_ref[:, cols]

    @pl.when(jnp.logical_not(match))
    def _():
        out_ref[...] = jnp.zeros(out_ref.shape, out_ref.dtype)


SMEM = pl.BlockSpec(memory_space=pltpu.SMEM)
HBM = pl.BlockSpec(memory_space=pltpu.HBM)
VMEM = pl.BlockSpec(memory_space=pltpu.VMEM)


def params(mib):
    return pltpu.CompilerParams(vmem_limit_bytes=mib * 1024 * 1024)


def stay(array):
    return pltpu.with_memory_space_constraint(array, pltpu.HBM)


def cost(flops, moved, powers=0):
    return pl.CostEstimate(flops=flops, bytes_accessed=moved, transcendentals=powers)


def near_attention(labels, mask, place, queries, keys, values):
    shard, width = queries.shape
    blocks = shard // BLOCK
    pieces = len(keys)
    piece_rows = keys[0].shape[0]
    rows = width // (KV_HEADS * HEAD_DIM) * BLOCK
    count = piece_rows * pieces
    state = jax.ShapeDtypeStruct((blocks, KV_HEADS, rows, LANES), F32)
    return pl.pallas_call(
        near_kernel,
        out_shape=[state, state, state, jax.ShapeDtypeStruct((blocks, BLOCK, width), BF16)],
        in_specs=[SMEM, SMEM, SMEM, HBM] + [VMEM] * (2 * pieces),
        out_specs=[VMEM] * 4,
        scratch_shapes=[
            pltpu.VMEM((blocks, pieces, piece_rows, BLOCK), BF16),
            pltpu.VMEM((2, rows, count), F32),
            pltpu.SemaphoreType.DMA((blocks,)),
        ],
        compiler_params=params(24),
        cost_estimate=cost(800 * shard * width * count, 2 * shard * width, shard * width // HEAD_DIM * count),
    )(labels, mask, place, queries, *keys, *values)


def far_attention(mode, first_piece, labels, mask, place, queries, residual, gains, state, keys, values, wg, wu, wd, after=()):
    blocks, tile, width = queries.shape
    pieces = len(keys)
    piece_rows = keys[0].shape[0]
    rows = width // (KV_HEADS * HEAD_DIM) * BLOCK
    count = piece_rows * pieces
    units = wg.shape[0]
    up_at = -(-units // LANES) * LANES
    taken = tile * (blocks if mode == WHOLE else 1)
    shape = jax.ShapeDtypeStruct
    outs = {
        LEAVE: [shape((tile // 2, width // CUTS), kind) for kind in (F32, BF16) for _ in range(CUTS)],
        STAY: [shape((tile // 2, width), F32), shape((tile // 2, units), BF16)],
        WHOLE: [shape((taken, width), F32)],
    }[mode]
    return pl.pallas_call(
        functools.partial(far_kernel, mode, first_piece, len(after)),
        out_shape=outs,
        in_specs=[SMEM, SMEM, SMEM, VMEM, HBM, VMEM] + [VMEM] * 3 + [pl.BlockSpec(memory_space=pl.ANY)] * len(after) + [VMEM] * (2 * pieces) + [HBM] * 3,
        out_specs=[VMEM] * len(outs),
        scratch_shapes=[
            pltpu.VMEM((taken, width), BF16),
            pltpu.VMEM((up_at + units, width), BF16),
            pltpu.VMEM(wd.shape, BF16),
            pltpu.VMEM((pieces, piece_rows, BLOCK), BF16),
            pltpu.VMEM((2, rows, count), F32),
            pltpu.VMEM((taken, width), BF16),
            pltpu.VMEM((taken, width), BF16),
            pltpu.VMEM((taken, units), BF16),
            pltpu.SemaphoreType.DMA((blocks,)),
            pltpu.SemaphoreType.DMA((3,)),
        ],
        compiler_params=params(30),
        cost_estimate=cost(
            (800 if mode == STAY else 1) * taken * width * count, width * units, taken * count
        ),
    )(labels, mask, place, queries, residual, gains, *state, *after, *keys, *values, wg, wu, wd)


def down_rest(labels, place, arrived, base, quarters):
    rows, width = base.shape
    units = arrived.shape[1]
    return pl.pallas_call(
        down_kernel,
        out_shape=jax.ShapeDtypeStruct((rows, width), F32),
        in_specs=[SMEM, SMEM] + [VMEM] * (2 + len(quarters)),
        out_specs=VMEM,
        compiler_params=params(16),
        cost_estimate=cost(rows * units, rows * units),
    )(labels, place, arrived, base, *quarters)


def xor_pairs(count, bits):
    return [(i, i ^ bits) for i in range(count)]


def per_device(queries, keys, values, residual, labels, block_mask, gains, w_gate, w_up, w_down):
    shard, width = queries.shape[1:]
    exp_count = lax.axis_size("exp")
    exp_here = lax.axis_index("exp")
    ctx_count = lax.axis_size("ctx")
    ctx_here = lax.axis_index("ctx")
    half = exp_count // 2
    split = exp_count == 4 and shard == 2 * BLOCK and ctx_count == 4 and lax.axis_size("dp") == 2
    section = exp_here // half
    low = exp_here % 2 if split else jnp.zeros_like(exp_here)
    core = ctx_here % 2
    first = exp_here % half == 0
    row = lax.axis_index("dp") % 2
    place = jnp.stack([value.astype(jnp.int32) for value in (ctx_here, section, low, core, first, row)])
    labels, block_mask, gains = stay(labels), stay(block_mask), stay(gains)
    own_q, own_res = stay(queries[0]), stay(residual[0])

    held = {0: (keys[0], values[0])}

    def spread(bits):
        pairs = xor_pairs(ctx_count, bits)
        for at, (k, v) in list(held.items()):
            held[at ^ bits] = (lax.ppermute(k, "ctx", pairs), lax.ppermute(v, "ctx", pairs))

    def swap(array):
        return lax.ppermute(array, "ctx", xor_pairs(ctx_count, 1))

    bits = ctx_count // 2
    while bits > 1:
        spread(bits)
        bits //= 2
    held[1] = (swap(keys[0]), swap(values[0]))
    *state, own_q = near_attention(
        labels, block_mask, place, own_q, [keys[0], held[1][0]], [values[0], held[1][1]]
    )
    if split:
        z_pairs = xor_pairs(exp_count, 1)
        cut = width // 4
        piece = lax.dynamic_slice_in_dim(w_down, (2 * row + core) * cut, cut, 1)
        quarter = lax.ppermute(piece, "exp", z_pairs)
    for at in range(2, ctx_count, 2):
        k, v = held[at]
        k, v, *state = lax.optimization_barrier((k, v, *state))
        held[at] = (k, v)
        held[at + 1] = (swap(k), swap(v))
    far = range(2, ctx_count)
    far_keys, far_values = [held[c][0] for c in far], [held[c][1] for c in far]
    shared = (labels, block_mask, place, own_q, own_res, gains)
    weights = (far_keys, far_values, stay(w_gate.T), stay(w_up.T), stay(w_down))
    if not split:
        (terms,) = far_attention(WHOLE, 2, *shared, state, *weights)
        return lax.psum_scatter(terms[None], "exp", scatter_dimension=1, tiled=True).astype(BF16)

    made = far_attention(LEAVE, 2, *shared, state, *weights)
    own_terms, sent = made[:CUTS], made[CUTS:]
    arrived = [lax.ppermute(part, "exp", z_pairs) for part in sent]
    leaving = [(mine + part.astype(F32)).astype(BF16) for mine, part in zip(own_terms, arrived)]
    crossed = [lax.ppermute(part, "exp", xor_pairs(exp_count, 2)) for part in leaving]

    quarter, _ = lax.optimization_barrier((quarter, sent[-1]))
    beside = lax.ppermute(quarter, "dp", xor_pairs(2, 1))
    quarters = [quarter, swap(quarter), beside, swap(beside)]
    base, send = far_attention(STAY, 2, *shared, state, *weights, after=leaving)
    staying = down_rest(labels, place, lax.ppermute(send, "exp", z_pairs), base, quarters)
    return (staying + jnp.concatenate(crossed, axis=1).astype(F32)).astype(BF16)[None]


def solution(mesh):
    placed = (
        P("dp", "ctx", None),
        P("dp", "ctx", None),
        P("dp", "ctx", None),
        P("dp", "ctx", None),
        P("dp", None),
        P("dp", None, None),
        P(),
        P(None, "exp"),
        P(None, "exp"),
        P("exp", None),
    )
    return jax.shard_map(
        per_device,
        mesh=mesh,
        in_specs=placed,
        out_specs=P("dp", ("ctx", "exp"), None),
        check_vma=False,
    )
```

```python
import functools

import jax
import jax.numpy as jnp
from jax import lax
from jax.experimental import pallas as pl
from jax.experimental.pallas import tpu as pltpu
from jax.sharding import PartitionSpec as P

KV_HEADS = 4
HEAD_DIM = 128
BLOCK = 128
LANES = 128
MASKED = -1e30
EXP2_SCALE = 1.4426950408889634 / (HEAD_DIM**0.5)
BF16 = jnp.bfloat16
F32 = jnp.float32
OVER_LAST = (((1,), (1,)), ((), ()))
WIDE = 256


def fill_bias(bias_ref, mask_ref, labels_ref, here, shards):
    key_in = lax.broadcasted_iota(jnp.int32, (BLOCK, BLOCK), 0)
    query_in = lax.broadcasted_iota(jnp.int32, (BLOCK, BLOCK), 1)
    later = (key_in > query_in).astype(jnp.int32)
    piece_blocks = bias_ref.shape[1] // BLOCK
    any_open = jnp.int32(0)
    for c, shard_of in enumerate(shards):
        for b in range(piece_blocks):
            other = shard_of * piece_blocks + b
            is_open = mask_ref[0, here, other]
            any_open = any_open | is_open
            closed = jnp.where(other == here, 1 - labels_ref[0, here], 0) * later
            closed = jnp.where(is_open == 1, closed, 1)
            bias_ref[c, b * BLOCK : (b + 1) * BLOCK, :] = jnp.where(closed == 1, MASKED, 0.0).astype(BF16)
    return any_open


def attend(q_ref, key_refs, value_refs, bias_ref, s_buf, prior, finish):
    tile, width = q_ref.shape
    group = width // (KV_HEADS * HEAD_DIM)
    rows = group * tile
    row_ids = lax.broadcasted_iota(jnp.int32, (tile, BLOCK), 0)
    col_ids = lax.broadcasted_iota(jnp.int32, (tile, BLOCK), 1)
    picks = jnp.where(row_ids == col_ids, 1.0, 0.0).astype(BF16)
    ones = jnp.ones((key_refs[0].shape[0], HEAD_DIM), BF16)
    limits = {}

    def score(g):
        q_all = jnp.concatenate(
            [
                jnp.concatenate([q_ref[:, (g * group + h) * HEAD_DIM : (g * group + h + 1) * HEAD_DIM], picks], axis=1)
                for h in range(group)
            ],
            axis=0,
        )
        lanes = slice(g * HEAD_DIM, (g + 1) * HEAD_DIM)
        k_all = jnp.concatenate(
            [jnp.concatenate([ref[:, lanes], bias_ref[c]], axis=1) for c, ref in enumerate(key_refs)], axis=0
        )
        s = lax.dot_general(q_all, k_all, OVER_LAST, preferred_element_type=F32)
        s_buf[g % 2] = s
        top = functools.reduce(jnp.maximum, [s[:, n : n + LANES] for n in range(0, s.shape[1], LANES)])
        top = jnp.broadcast_to(jnp.max(top, axis=1, keepdims=True), (rows, LANES))
        if prior is not None:
            top = jnp.maximum(top, prior(g)[2])
        limits[g] = top

    def mix(g):
        lanes = slice(g * HEAD_DIM, (g + 1) * HEAD_DIM)
        shift = limits[g] * EXP2_SCALE
        soft = jnp.concatenate(
            [
                jnp.exp2(s_buf[g % 2, :, n : n + LANES] * EXP2_SCALE - shift).astype(BF16)
                for n in range(0, s_buf.shape[2], LANES)
            ],
            axis=1,
        )
        v_all = jnp.concatenate([jnp.concatenate([ref[:, lanes], ones], axis=1) for ref in value_refs], axis=0)
        mixed = jnp.dot(soft, v_all, preferred_element_type=F32)
        sums, totals = mixed[:, :HEAD_DIM], mixed[:, HEAD_DIM:]
        if prior is not None:
            before = prior(g)
            factor = jnp.exp2((before[2] - limits[g]) * EXP2_SCALE)
            sums = sums + before[0] * factor
            totals = totals + before[1] * factor
        finish(g, sums, totals, limits[g])

    score(0)
    for g in range(KV_HEADS):
        if g + 1 < KV_HEADS:
            score(g + 1)
        mix(g)


def quarters_kernel(place_ref, wd_hbm, *rest):
    out_refs, sem = rest[:-1], rest[-1]
    low, core = place_ref[2], place_ref[3]
    width = wd_hbm.shape[1]
    copies = []
    for i, half in enumerate((1 - low, low)):
        cols = pl.ds(pl.multiple_of(half * (width // 2) + core * (width // 4), LANES), width // 4)
        copies.append(pltpu.make_async_copy(wd_hbm.at[:, cols], out_refs[i], sem.at[i]))
    for copy in copies:
        copy.start()
    for copy in copies:
        copy.wait()


def near_kernel(split, labels_ref, mask_ref, place_ref, q_hbm, k_hbm, v_hbm, k_ref, v_ref, *rest):
    k_buf, v_buf, bias_buf, s_buf, sem, kv_sem = rest[-6:]
    blocks = len(rest[:-6]) // 4
    outs = [rest[4 * i : 4 * i + 4] for i in range(blocks)]
    tile = outs[0][3].shape[0]
    ctx_here, section = place_ref[0], place_ref[1]
    order = [1 - section, section] if split else list(range(blocks))

    loads = [
        pltpu.make_async_copy(q_hbm.at[pl.ds(pl.multiple_of(t * tile, tile), tile)], outs[i][3], sem.at[i])
        for i, t in enumerate(order)
    ]
    loads.append(pltpu.make_async_copy(k_hbm, k_buf, kv_sem.at[0]))
    loads.append(pltpu.make_async_copy(v_hbm, v_buf, kv_sem.at[1]))
    for copy in loads:
        copy.start()
    for i, t in enumerate(order):
        fill_bias(bias_buf.at[i], mask_ref, labels_ref, ctx_here * blocks + t, [ctx_here, ctx_here ^ 1])
    for copy in loads:
        copy.wait()

    for i, t in enumerate(order):
        sums_ref, totals_ref, limits_ref, q_ref = outs[i]

        @pl.when(labels_ref[0, ctx_here * blocks + t] == section)
        def _():
            def finish(g, sums, totals, limit):
                sums_ref[g] = sums
                totals_ref[g] = totals
                limits_ref[g] = limit

            attend(q_ref, [k_buf, k_ref], [v_buf, v_ref], bias_buf.at[i], s_buf, None, finish)


def attend_far(match, here, pieces, refs, att_ref, bias_buf, s_buf):
    labels_ref, mask_ref, place_ref, key_refs, value_refs, sums_ref, totals_ref, limits_ref, q_ref = refs
    tile, width = att_ref.shape
    group = width // (KV_HEADS * HEAD_DIM)
    opened = fill_bias(bias_buf, mask_ref, labels_ref, here, [place_ref[0] ^ c for c in pieces])

    def finish(g, sums, totals, _):
        attended = (sums / totals).astype(BF16)
        for h in range(group):
            at = (g * group + h) * HEAD_DIM
            att_ref[:, at : at + HEAD_DIM] = attended[h * tile : (h + 1) * tile]

    def prior(g):
        return sums_ref[g], totals_ref[g], limits_ref[g]

    @pl.when(match & (opened > 0))
    def _():
        attend(q_ref, key_refs, value_refs, bias_buf, s_buf, prior, finish)

    @pl.when(match & (opened == 0))
    def _():
        for g in range(KV_HEADS):
            finish(g, sums_ref[g], totals_ref[g], None)


def norm_block(gains_ref, section, first_row, tile, mid_of, norm_buf):
    gain = gains_ref[pl.ds(section, 1), :]
    step = 16

    def norm_rows(j, carry):
        rows = pl.ds(pl.multiple_of(first_row + j * step, step), step)
        mid = mid_of(rows, slice(None))
        factor = lax.rsqrt(jnp.mean(mid * mid, axis=-1, keepdims=True) + 1e-05)
        norm_buf[rows, :] = (mid * factor * gain).astype(BF16)
        return carry

    lax.fori_loop(0, tile // step, norm_rows, 0)


def hidden_of(norm_buf, w_ref, units):
    up_at = w_ref.shape[0] - units
    both = lax.dot_general(norm_buf[...], w_ref[...], OVER_LAST, preferred_element_type=F32)
    gate, upper = both[:, :units], both[:, up_at : up_at + units]
    return (gate * upper / (1.0 + jnp.exp(-gate))).astype(BF16)


def halves_of(place_ref, tile):
    half = tile // 2
    low = place_ref[2]
    own = pl.ds(pl.multiple_of(low * half, half), half)
    return own, pl.ds(pl.multiple_of(half - low * half, half), half)


def far_kernel(split, pieces, labels_ref, mask_ref, place_ref, res_hbm, gains_ref, *rest):
    tile, width = rest[3].shape
    blocks = res_hbm.shape[0] // tile
    state_refs, rest = rest[: 4 * blocks], rest[4 * blocks :]
    count = len(pieces)
    key_refs, value_refs = rest[:count], rest[count : 2 * count]
    wg_hbm, wu_hbm, wd_hbm = rest[2 * count : 2 * count + 3]
    out_refs = rest[2 * count + 3 : -10]
    res_buf, w_buf, wd_buf, bias_buf, s_buf, att_buf, norm_buf, hid_buf, sem, w_sem = rest[-10:]
    units = wg_hbm.shape[0]
    ctx_here, section, first = place_ref[0], place_ref[1], place_ref[4]
    chosen = [1 - section, section] if split else list(range(blocks))
    refs = (labels_ref, mask_ref, place_ref, key_refs, value_refs)

    loads = []
    for i, t in enumerate(chosen):
        rows = pl.ds(pl.multiple_of(t * tile, tile), tile)
        loads.append(pltpu.make_async_copy(res_hbm.at[rows], res_buf.at[pl.ds(i * tile, tile)], sem.at[i]))
    loads.append(pltpu.make_async_copy(wg_hbm, w_buf.at[pl.ds(0, units)], w_sem.at[0]))
    loads.append(pltpu.make_async_copy(wu_hbm, w_buf.at[pl.ds(w_buf.shape[0] - units, units)], w_sem.at[1]))
    later = pltpu.make_async_copy(wd_hbm, wd_buf, w_sem.at[2])
    for copy in loads:
        copy.start()
    later.start()

    matches = [labels_ref[0, ctx_here * blocks + t] == section for t in chosen]
    for i, t in enumerate(chosen):
        span = pl.ds(i * tile, tile)
        block_refs = (*refs, *state_refs[4 * i : 4 * i + 4])
        attend_far(matches[i], ctx_here * blocks + t, pieces, block_refs, att_buf.at[span], bias_buf, s_buf)

        @pl.when(jnp.logical_not(matches[i]))
        def _():
            norm_buf[span, :] = jnp.zeros((tile, width), BF16)

    for copy in loads:
        copy.wait()

    def mid_of(rows, cols):
        return res_buf[rows, cols].astype(F32) + att_buf[rows, cols].astype(F32)

    for i in range(len(chosen)):

        @pl.when(matches[i])
        def _():
            norm_block(gains_ref, section, i * tile, tile, mid_of, norm_buf)

    later.wait()

    @pl.when(functools.reduce(jnp.logical_or, matches))
    def _():
        hid_buf[...] = hidden_of(norm_buf, w_buf, units)
        if split:
            send_ref, keep_ref, terms_ref, mid_ref = out_refs
            own, other = [pl.ds(pl.multiple_of(span.start + tile, span.size), span.size) for span in halves_of(place_ref, tile)]
            send_ref[:tile, :] = hid_buf[:tile, :]
            send_ref[tile:, :] = hid_buf[other, :]
            keep_ref[...] = hid_buf[own, :]
            for n in range(0, width // 2, WIDE):
                cols = pl.ds(pl.multiple_of(place_ref[2] * (width // 2) + n, LANES), WIDE)
                terms = jnp.dot(hid_buf[:tile, :], wd_buf[:, cols], preferred_element_type=F32)
                terms_ref[:, n : n + WIDE] = terms + mid_of(slice(0, tile), cols)
            for n in range(0, width, WIDE):
                mid_ref[:, n : n + WIDE] = mid_of(own, slice(n, n + WIDE))
        else:
            for n in range(0, width, WIDE):
                cols = slice(n, n + WIDE)
                terms = jnp.dot(hid_buf[...], wd_buf[:, cols], preferred_element_type=F32)
                for i in range(blocks):
                    span = slice(i * tile, (i + 1) * tile)
                    kept = terms[span] + mid_of(span, cols) * first.astype(F32)
                    out_refs[0][span, cols] = jnp.where(matches[i], kept, 0.0)

    if not split:

        @pl.when(jnp.logical_not(functools.reduce(jnp.logical_or, matches)))
        def _():
            out_refs[0][...] = jnp.zeros(out_refs[0].shape, F32)


def down_leave_kernel(labels_ref, place_ref, in_ref, base_ref, here_ref, there_ref, after_ref, same_ref, other_ref, token_ref):
    tile, quarter = base_ref.shape[0], here_ref.shape[1]
    ctx_here, section, core = place_ref[0], place_ref[1], place_ref[3]
    match = labels_ref[0, ctx_here * 2 + 1 - section] == section
    token_ref[...] = jnp.zeros(token_ref.shape, F32)
    rows = halves_of(place_ref, tile)

    @pl.when(match)
    def _():
        left = jnp.concatenate([in_ref[span, :] for span in rows], axis=0)
        for from_core, ref in ((core, here_ref), (1 - core, there_ref)):
            for n in range(0, quarter, WIDE):
                wide = min(WIDE, quarter - n)
                cols = pl.ds(pl.multiple_of(from_core * quarter + n, LANES), wide)
                terms = jnp.dot(left, ref[:, n : n + wide], preferred_element_type=F32)
                for i, to_ref in enumerate((same_ref, other_ref)):
                    part = terms[i * tile // 2 : (i + 1) * tile // 2] + base_ref[rows[i], cols]
                    to_ref[:, cols] = part.astype(BF16)

    @pl.when(jnp.logical_not(match))
    def _():
        same_ref[...] = jnp.zeros(same_ref.shape, BF16)
        other_ref[...] = jnp.zeros(other_ref.shape, BF16)


def down_stay_kernel(labels_ref, place_ref, in_ref, keep_ref, mid_ref, after_ref, wd_hbm, *rest):
    quarter_refs, (out_ref, wd_buf, sem) = rest[:-3], rest[-3:]
    quarter = quarter_refs[0].shape[1]
    rows = keep_ref.shape[0]
    ctx_here, section, low, core = place_ref[0], place_ref[1], place_ref[2], place_ref[3]
    match = labels_ref[0, ctx_here * 2 + section] == section

    @pl.when(match)
    def _():
        copy = pltpu.make_async_copy(wd_hbm, wd_buf, sem)
        copy.start()
        copy.wait()
        arrived = in_ref[in_ref.shape[0] - rows :, :]
        for i, ref in enumerate(quarter_refs):
            half = low if i < 2 else 1 - low
            from_core = core if i % 2 == 0 else 1 - core
            for n in range(0, quarter, WIDE):
                wide = min(WIDE, quarter - n)
                cols = pl.ds(pl.multiple_of((2 * half + from_core) * quarter + n, LANES), wide)
                terms = jnp.dot(arrived, ref[:, n : n + wide], preferred_element_type=F32)
                terms = terms + jnp.dot(keep_ref[...], wd_buf[:, cols], preferred_element_type=F32)
                out_ref[:, cols] = terms + mid_ref[:, cols]

    @pl.when(jnp.logical_not(match))
    def _():
        out_ref[...] = jnp.zeros(out_ref.shape, F32)


def last_sum_kernel(place_ref, staying_ref, same_ref, other_ref, out_ref):
    half = same_ref.shape[1]
    low = place_ref[2]
    for at, ref in ((low, same_ref), (1 - low, other_ref)):
        for n in range(0, half, WIDE):
            cols = pl.ds(pl.multiple_of(at * half + n, LANES), WIDE)
            out_ref[:, cols] = (staying_ref[:, cols] + ref[:, n : n + WIDE].astype(F32)).astype(BF16)


SMEM = pl.BlockSpec(memory_space=pltpu.SMEM)
HBM = pl.BlockSpec(memory_space=pltpu.HBM)
VMEM = pl.BlockSpec(memory_space=pltpu.VMEM)
ANY = pl.BlockSpec(memory_space=pl.ANY)


def params(mib):
    return pltpu.CompilerParams(vmem_limit_bytes=mib * 1024 * 1024)


def stay(array):
    return pltpu.with_memory_space_constraint(array, pltpu.HBM)


def cost(flops, moved, powers=0):
    return pl.CostEstimate(flops=flops, bytes_accessed=moved, transcendentals=powers)


def w_down_quarters(place, wd):
    units, width = wd.shape
    return pl.pallas_call(
        quarters_kernel,
        out_shape=[jax.ShapeDtypeStruct((units, width // 4), BF16)] * 2,
        in_specs=[SMEM, HBM],
        out_specs=[VMEM] * 2,
        scratch_shapes=[pltpu.SemaphoreType.DMA((2,))],
        compiler_params=params(8),
        cost_estimate=cost(units, units * width),
    )(place, wd)


def near_attention(split, labels, mask, place, queries, own_key, own_value, key, value):
    shard, width = queries.shape
    blocks = shard // BLOCK
    piece_rows, kv_width = key.shape
    rows = width // (KV_HEADS * HEAD_DIM) * BLOCK
    count = 2 * piece_rows
    shape = jax.ShapeDtypeStruct
    state = shape((KV_HEADS, rows, LANES), F32)
    outs = [state, state, state, shape((BLOCK, width), BF16)] * blocks
    made = pl.pallas_call(
        functools.partial(near_kernel, split),
        out_shape=outs,
        in_specs=[SMEM, SMEM, SMEM, HBM, HBM, HBM, VMEM, VMEM],
        out_specs=[VMEM] * len(outs),
        scratch_shapes=[
            pltpu.VMEM((piece_rows, kv_width), BF16),
            pltpu.VMEM((piece_rows, kv_width), BF16),
            pltpu.VMEM((blocks, 2, piece_rows, BLOCK), BF16),
            pltpu.VMEM((2, rows, count), F32),
            pltpu.SemaphoreType.DMA((blocks,)),
            pltpu.SemaphoreType.DMA((2,)),
        ],
        compiler_params=params(16),
        cost_estimate=cost(800 * shard * width * count, 2 * shard * width, shard * width // HEAD_DIM * count),
    )(labels, mask, place, queries, own_key, own_value, key, value)
    return [list(made[4 * i : 4 * i + 4]) for i in range(blocks)]


def far_attention(split, pieces, labels, mask, place, residual, gains, states, keys, values, wg, wu, wd):
    tile, width = states[0][3].shape
    piece_rows = keys[0].shape[0]
    rows = width // (KV_HEADS * HEAD_DIM) * BLOCK
    count = piece_rows * len(pieces)
    units = wg.shape[0]
    up_at = -(-units // LANES) * LANES
    taken = tile * len(states)
    shape = jax.ShapeDtypeStruct
    if split:
        outs = [shape((tile + tile // 2, units), BF16), shape((tile // 2, units), BF16)]
        outs += [shape((tile, width // 2), F32), shape((tile // 2, width), F32)]
    else:
        outs = [shape((taken, width), F32)]
    return pl.pallas_call(
        functools.partial(far_kernel, split, pieces),
        out_shape=outs,
        in_specs=[SMEM, SMEM, SMEM, HBM, VMEM] + [VMEM] * (4 * len(states) + 2 * len(pieces)) + [HBM] * 3,
        out_specs=[VMEM] * len(outs),
        scratch_shapes=[
            pltpu.VMEM((taken, width), BF16),
            pltpu.VMEM((up_at + units, width), BF16),
            pltpu.VMEM(wd.shape, BF16),
            pltpu.VMEM((len(pieces), piece_rows, BLOCK), BF16),
            pltpu.VMEM((2, rows, count), F32),
            pltpu.VMEM((taken, width), BF16),
            pltpu.VMEM((taken, width), BF16),
            pltpu.VMEM((taken, units), BF16),
            pltpu.SemaphoreType.DMA((len(states),)),
            pltpu.SemaphoreType.DMA((3,)),
        ],
        compiler_params=params(28),
        cost_estimate=cost(taken * width, width, taken),
    )(
        labels, mask, place, residual, gains, *[array for state in states for array in state],
        *keys, *values, wg, wu, wd,
    )


TOKEN = jax.ShapeDtypeStruct((8, LANES), F32)


def down_leave(labels, place, arrived, base, here, there, after):
    tile, half_width = base.shape
    half = jax.ShapeDtypeStruct((tile // 2, half_width), BF16)
    return pl.pallas_call(
        down_leave_kernel,
        out_shape=[half, half, TOKEN],
        in_specs=[SMEM, SMEM] + [VMEM] * 4 + [ANY],
        out_specs=[VMEM] * 3,
        compiler_params=params(16),
        cost_estimate=cost(tile, tile),
    )(labels, place, arrived, base, here, there, after)


def down_stay(labels, place, arrived, keep, mid, after, wd, *quarters):
    rows, units = keep.shape
    return pl.pallas_call(
        down_stay_kernel,
        out_shape=jax.ShapeDtypeStruct(mid.shape, F32),
        in_specs=[SMEM, SMEM, VMEM, VMEM, VMEM, ANY, HBM] + [VMEM] * len(quarters),
        out_specs=VMEM,
        scratch_shapes=[pltpu.VMEM(wd.shape, BF16), pltpu.SemaphoreType.DMA(())],
        compiler_params=params(16),
        cost_estimate=cost(8000 * rows * wd.size, wd.size),
    )(labels, place, arrived, keep, mid, after, wd, *quarters)


def last_sum(place, staying, same, other):
    return pl.pallas_call(
        last_sum_kernel,
        out_shape=jax.ShapeDtypeStruct(staying.shape, BF16),
        in_specs=[SMEM] + [VMEM] * 3,
        out_specs=VMEM,
        compiler_params=params(8),
        cost_estimate=cost(staying.size, staying.size),
    )(place, staying, same, other)


def xor_pairs(count, bits):
    return [(i, i ^ bits) for i in range(count)]


def per_device(queries, keys, values, residual, labels, block_mask, gains, w_gate, w_up, w_down):
    shard, width = queries.shape[1:]
    exp_count = lax.axis_size("exp")
    exp_here = lax.axis_index("exp")
    ctx_count = lax.axis_size("ctx")
    ctx_here = lax.axis_index("ctx")
    half = exp_count // 2
    split = exp_count == 4 and shard == 2 * BLOCK and ctx_count == 4
    section = exp_here // half
    low = exp_here % 2 if split else jnp.zeros_like(exp_here)
    core = ctx_here % 2
    first = exp_here % half == 0
    place = jnp.stack([value.astype(jnp.int32) for value in (ctx_here, section, low, core, first)])
    labels, block_mask, gains = stay(labels), stay(block_mask), stay(gains)
    own_q, own_res = stay(queries[0]), stay(residual[0])

    held = {0: (keys[0], values[0])}

    def spread(bits):
        pairs = xor_pairs(ctx_count, bits)
        for at, (k, v) in list(held.items()):
            held[at ^ bits] = (lax.ppermute(k, "ctx", pairs), lax.ppermute(v, "ctx", pairs))

    def swap(array):
        return lax.ppermute(array, "ctx", xor_pairs(ctx_count, 1))

    bits = ctx_count // 2
    while bits > 1:
        spread(bits)
        bits //= 2
    held[1] = (swap(keys[0]), swap(values[0]))
    z_pairs = xor_pairs(exp_count, 1)
    if split:
        here, late = w_down_quarters(place, stay(w_down))
        late, key = lax.optimization_barrier((late, held[1][0]))
        held[1] = (key, held[1][1])
        here, late = lax.ppermute(here, "exp", z_pairs), lax.ppermute(late, "exp", z_pairs)
    states = near_attention(
        split, labels, block_mask, place, own_q, stay(keys[0]), stay(values[0]), *held[1]
    )
    for at in range(2, ctx_count, 2):
        k, v = held[at]
        k, v, states[0][0] = lax.optimization_barrier((k, v, states[0][0]))
        held[at] = (k, v)
        held[at + 1] = (swap(k), swap(v))
    far = range(2, ctx_count)
    far_keys, far_values = [held[c][0] for c in far], [held[c][1] for c in far]
    weights = (far_keys, far_values, stay(w_gate.T), stay(w_up.T), stay(w_down))
    shared = (labels, block_mask, place, own_res, gains)
    made = far_attention(split, far, *shared, states, *weights)
    if not split:
        return lax.psum_scatter(made[0][None], "exp", scatter_dimension=1, tiled=True).astype(BF16)

    send, keep, base, mid = made
    here, send = lax.optimization_barrier((here, send))
    there = swap(here)
    arrived = lax.ppermute(send, "exp", z_pairs)
    same, other, token = down_leave(labels, place, arrived, base, here, there, late)
    late, token = lax.optimization_barrier((late, token))
    same, other = (
        lax.ppermute(part, "exp", xor_pairs(exp_count, bits)) for part, bits in ((same, 2), (other, 3))
    )
    staying = down_stay(labels, place, arrived, keep, mid, token, stay(w_down), here, there, late, swap(late))
    return last_sum(place, staying, same, other)[None]


def solution(mesh):
    placed = (
        P("dp", "ctx", None),
        P("dp", "ctx", None),
        P("dp", "ctx", None),
        P("dp", "ctx", None),
        P("dp", None),
        P("dp", None, None),
        P(),
        P(None, "exp"),
        P(None, "exp"),
        P("exp", None),
    )
    return jax.shard_map(
        per_device,
        mesh=mesh,
        in_specs=placed,
        out_specs=P("dp", ("ctx", "exp"), None),
        check_vma=False,
    )
```

```python
import functools

import jax
import jax.numpy as jnp
from jax import lax
from jax.experimental import pallas as pl
from jax.experimental.pallas import tpu as pltpu
from jax.sharding import PartitionSpec as P

KV_HEADS = 4
HEAD_DIM = 128
BLOCK = 128
LANES = 128
MASKED = -1e30
EXP2_SCALE = 1.4426950408889634 / (HEAD_DIM**0.5)
BF16 = jnp.bfloat16
F32 = jnp.float32
OVER_LAST = (((1,), (1,)), ((), ()))
WIDE = 256


def fill_bias(bias_ref, mask_ref, labels_ref, here, shards):
    key_in = lax.broadcasted_iota(jnp.int32, (BLOCK, BLOCK), 0)
    query_in = lax.broadcasted_iota(jnp.int32, (BLOCK, BLOCK), 1)
    later = (key_in > query_in).astype(jnp.int32)
    piece_blocks = bias_ref.shape[1] // BLOCK
    any_open = jnp.int32(0)
    for c, shard_of in enumerate(shards):
        for b in range(piece_blocks):
            other = shard_of * piece_blocks + b
            is_open = mask_ref[0, here, other]
            any_open = any_open | is_open
            closed = jnp.where(other == here, 1 - labels_ref[0, here], 0) * later
            closed = jnp.where(is_open == 1, closed, 1)
            bias_ref[c, b * BLOCK : (b + 1) * BLOCK, :] = jnp.where(closed == 1, MASKED, 0.0).astype(BF16)
    return any_open


def attend(q_ref, key_refs, value_refs, bias_ref, s_buf, prior, finish):
    tile, width = q_ref.shape
    group = width // (KV_HEADS * HEAD_DIM)
    rows = group * tile
    row_ids = lax.broadcasted_iota(jnp.int32, (tile, BLOCK), 0)
    col_ids = lax.broadcasted_iota(jnp.int32, (tile, BLOCK), 1)
    picks = jnp.where(row_ids == col_ids, 1.0, 0.0).astype(BF16)
    ones = jnp.ones((key_refs[0].shape[0], HEAD_DIM), BF16)
    limits = {}

    def score(g):
        q_all = jnp.concatenate(
            [
                jnp.concatenate([q_ref[:, (g * group + h) * HEAD_DIM : (g * group + h + 1) * HEAD_DIM], picks], axis=1)
                for h in range(group)
            ],
            axis=0,
        )
        lanes = slice(g * HEAD_DIM, (g + 1) * HEAD_DIM)
        k_all = jnp.concatenate(
            [jnp.concatenate([ref[:, lanes], bias_ref[c]], axis=1) for c, ref in enumerate(key_refs)], axis=0
        )
        s = lax.dot_general(q_all, k_all, OVER_LAST, preferred_element_type=F32)
        s_buf[g % 2] = s
        top = functools.reduce(jnp.maximum, [s[:, n : n + LANES] for n in range(0, s.shape[1], LANES)])
        top = jnp.broadcast_to(jnp.max(top, axis=1, keepdims=True), (rows, LANES))
        if prior is not None:
            top = jnp.maximum(top, prior(g)[2])
        limits[g] = top

    def mix(g):
        lanes = slice(g * HEAD_DIM, (g + 1) * HEAD_DIM)
        shift = limits[g] * EXP2_SCALE
        soft = jnp.concatenate(
            [
                jnp.exp2(s_buf[g % 2, :, n : n + LANES] * EXP2_SCALE - shift).astype(BF16)
                for n in range(0, s_buf.shape[2], LANES)
            ],
            axis=1,
        )
        v_all = jnp.concatenate([jnp.concatenate([ref[:, lanes], ones], axis=1) for ref in value_refs], axis=0)
        mixed = jnp.dot(soft, v_all, preferred_element_type=F32)
        sums, totals = mixed[:, :HEAD_DIM], mixed[:, HEAD_DIM:]
        if prior is not None:
            before = prior(g)
            factor = jnp.exp2((before[2] - limits[g]) * EXP2_SCALE)
            sums = sums + before[0] * factor
            totals = totals + before[1] * factor
        finish(g, sums, totals, limits[g])

    score(0)
    for g in range(KV_HEADS):
        if g + 1 < KV_HEADS:
            score(g + 1)
        mix(g)


def quarter_kernel(place_ref, wd_hbm, out_ref, sem):
    low, core = place_ref[2], place_ref[3]
    width = wd_hbm.shape[1]
    cols = pl.ds(pl.multiple_of((1 - low) * (width // 2) + core * (width // 4), LANES), width // 4)
    copy = pltpu.make_async_copy(wd_hbm.at[:, cols], out_ref, sem)
    copy.start()
    copy.wait()


def near_kernel(split, labels_ref, mask_ref, place_ref, q_hbm, k_hbm, v_hbm, k_ref, v_ref, *rest):
    k_buf, v_buf, bias_buf, s_buf, sem, kv_sem = rest[-6:]
    blocks = len(rest[:-6]) // 4
    outs = [rest[4 * i : 4 * i + 4] for i in range(blocks)]
    tile = outs[0][3].shape[0]
    ctx_here, section = place_ref[0], place_ref[1]
    order = [1 - section, section] if split else list(range(blocks))

    loads = [
        pltpu.make_async_copy(q_hbm.at[pl.ds(pl.multiple_of(t * tile, tile), tile)], outs[i][3], sem.at[i])
        for i, t in enumerate(order)
    ]
    loads.append(pltpu.make_async_copy(k_hbm, k_buf, kv_sem.at[0]))
    loads.append(pltpu.make_async_copy(v_hbm, v_buf, kv_sem.at[1]))
    for copy in loads:
        copy.start()
    for i, t in enumerate(order):
        fill_bias(bias_buf.at[i], mask_ref, labels_ref, ctx_here * blocks + t, [ctx_here, ctx_here ^ 1])
    for copy in loads:
        copy.wait()

    for i, t in enumerate(order):
        sums_ref, totals_ref, limits_ref, q_ref = outs[i]

        @pl.when(labels_ref[0, ctx_here * blocks + t] == section)
        def _():
            def finish(g, sums, totals, limit):
                sums_ref[g] = sums
                totals_ref[g] = totals
                limits_ref[g] = limit

            attend(q_ref, [k_buf, k_ref], [v_buf, v_ref], bias_buf.at[i], s_buf, None, finish)


def attend_far(match, here, pieces, refs, att_ref, bias_buf, s_buf):
    labels_ref, mask_ref, place_ref, key_refs, value_refs, sums_ref, totals_ref, limits_ref, q_ref = refs
    tile, width = att_ref.shape
    group = width // (KV_HEADS * HEAD_DIM)
    opened = fill_bias(bias_buf, mask_ref, labels_ref, here, [place_ref[0] ^ c for c in pieces])

    def finish(g, sums, totals, _):
        attended = (sums / totals).astype(BF16)
        for h in range(group):
            at = (g * group + h) * HEAD_DIM
            att_ref[:, at : at + HEAD_DIM] = attended[h * tile : (h + 1) * tile]

    def prior(g):
        return sums_ref[g], totals_ref[g], limits_ref[g]

    @pl.when(match & (opened > 0))
    def _():
        attend(q_ref, key_refs, value_refs, bias_buf, s_buf, prior, finish)

    @pl.when(match & (opened == 0))
    def _():
        for g in range(KV_HEADS):
            finish(g, sums_ref[g], totals_ref[g], None)


def norm_block(gains_ref, section, first_row, tile, mid_of, norm_buf):
    gain = gains_ref[pl.ds(section, 1), :]
    step = 16

    def norm_rows(j, carry):
        rows = pl.ds(pl.multiple_of(first_row + j * step, step), step)
        mid = mid_of(rows, slice(None))
        factor = lax.rsqrt(jnp.mean(mid * mid, axis=-1, keepdims=True) + 1e-05)
        norm_buf[rows, :] = (mid * factor * gain).astype(BF16)
        return carry

    lax.fori_loop(0, tile // step, norm_rows, 0)


def hidden_of(norm_buf, w_ref, units):
    up_at = w_ref.shape[0] - units
    both = lax.dot_general(norm_buf[...], w_ref[...], OVER_LAST, preferred_element_type=F32)
    gate, upper = both[:, :units], both[:, up_at : up_at + units]
    return (gate * upper / (1.0 + jnp.exp(-gate))).astype(BF16)


def halves_of(place_ref, tile):
    half = tile // 2
    low = place_ref[2]
    own = pl.ds(pl.multiple_of(low * half, half), half)
    return own, pl.ds(pl.multiple_of(half - low * half, half), half)


def far_kernel(split, pieces, labels_ref, mask_ref, place_ref, res_hbm, gains_ref, *rest):
    tile, width = rest[3].shape
    blocks = res_hbm.shape[0] // tile
    state_refs, rest = rest[: 4 * blocks], rest[4 * blocks :]
    count = len(pieces)
    key_refs, value_refs = rest[:count], rest[count : 2 * count]
    wg_hbm, wu_hbm, wd_hbm = rest[2 * count : 2 * count + 3]
    out_refs = rest[2 * count + 3 : -10]
    res_buf, w_buf, wd_buf, bias_buf, s_buf, att_buf, norm_buf, hid_buf, sem, w_sem = rest[-10:]
    if split:
        send_ref, hid_ref, mid_ref, wd_buf, sent_ref = out_refs
    units = wg_hbm.shape[0]
    ctx_here, section, first = place_ref[0], place_ref[1], place_ref[4]
    chosen = [1 - section, section] if split else list(range(blocks))
    refs = (labels_ref, mask_ref, place_ref, key_refs, value_refs)

    loads = []
    for i, t in enumerate(chosen):
        rows = pl.ds(pl.multiple_of(t * tile, tile), tile)
        loads.append(pltpu.make_async_copy(res_hbm.at[rows], res_buf.at[pl.ds(i * tile, tile)], sem.at[i]))
    loads.append(pltpu.make_async_copy(wg_hbm, w_buf.at[pl.ds(0, units)], w_sem.at[0]))
    loads.append(pltpu.make_async_copy(wu_hbm, w_buf.at[pl.ds(w_buf.shape[0] - units, units)], w_sem.at[1]))
    later = pltpu.make_async_copy(wd_hbm, wd_buf, w_sem.at[2])
    for copy in loads:
        copy.start()
    later.start()

    matches = [labels_ref[0, ctx_here * blocks + t] == section for t in chosen]
    for i, t in enumerate(chosen):
        span = pl.ds(i * tile, tile)
        block_refs = (*refs, *state_refs[4 * i : 4 * i + 4])
        attend_far(matches[i], ctx_here * blocks + t, pieces, block_refs, att_buf.at[span], bias_buf, s_buf)

        @pl.when(jnp.logical_not(matches[i]))
        def _():
            norm_buf[span, :] = jnp.zeros((tile, width), BF16)

    for copy in loads:
        copy.wait()

    def mid_of(rows, cols):
        mid = res_buf[rows, cols].astype(F32) + att_buf[rows, cols].astype(F32)
        if split:
            mid_ref[rows, cols] = mid
        return mid

    for i in range(len(chosen)):

        @pl.when(matches[i])
        def _():
            norm_block(gains_ref, section, i * tile, tile, mid_of, norm_buf)

    later.wait()

    @pl.when(functools.reduce(jnp.logical_or, matches))
    def _():
        hid_buf[...] = hidden_of(norm_buf, w_buf, units)
        if split:
            other = halves_of(place_ref, tile)[1]
            other = pl.ds(pl.multiple_of(other.start + tile, other.size), other.size)
            hid_ref[...] = hid_buf[...]
            send_ref[:tile, :] = hid_buf[:tile, :]
            send_ref[tile:, :] = hid_buf[other, :]

            @pl.when(matches[1])
            def _():
                for n in range(0, width // 2, WIDE):
                    cols = pl.ds(pl.multiple_of(place_ref[2] * (width // 2) + n, LANES), WIDE)
                    terms = jnp.dot(hid_buf[other, :], wd_buf[:, cols], preferred_element_type=F32)
                    sent_ref[:, n : n + WIDE] = terms.astype(BF16)

        else:
            for n in range(0, width, WIDE):
                cols = slice(n, n + WIDE)
                terms = jnp.dot(hid_buf[...], wd_buf[:, cols], preferred_element_type=F32)
                for i in range(blocks):
                    span = slice(i * tile, (i + 1) * tile)
                    kept = terms[span] + mid_of(span, cols) * first.astype(F32)
                    out_refs[0][span, cols] = jnp.where(matches[i], kept, 0.0)

    if not split:

        @pl.when(jnp.logical_not(functools.reduce(jnp.logical_or, matches)))
        def _():
            out_refs[0][...] = jnp.zeros(out_refs[0].shape, F32)


def down_own_kernel(labels_ref, place_ref, hid_ref, mid_ref, wd_ref, out_ref):
    tile, half = out_ref.shape
    ctx_here, section, low = place_ref[0], place_ref[1], place_ref[2]

    @pl.when(labels_ref[0, ctx_here * 2 + 1 - section] == section)
    def _():
        for n in range(0, half, WIDE):
            cols = pl.ds(pl.multiple_of(low * half + n, LANES), WIDE)
            terms = jnp.dot(hid_ref[:tile, :], wd_ref[:, cols], preferred_element_type=F32)
            out_ref[:, n : n + WIDE] = terms + mid_ref[:tile, cols]


def down_leave_kernel(labels_ref, place_ref, in_ref, base_ref, here_ref, there_ref, same_ref, other_ref, token_ref):
    tile, quarter = base_ref.shape[0], here_ref.shape[1]
    ctx_here, section, core = place_ref[0], place_ref[1], place_ref[3]
    match = labels_ref[0, ctx_here * 2 + 1 - section] == section
    token_ref[...] = jnp.zeros(token_ref.shape, F32)
    rows = halves_of(place_ref, tile)

    @pl.when(match)
    def _():
        left = jnp.concatenate([in_ref[span, :] for span in rows], axis=0)
        for from_core, ref in ((core, here_ref), (1 - core, there_ref)):
            for n in range(0, quarter, WIDE):
                wide = min(WIDE, quarter - n)
                cols = pl.ds(pl.multiple_of(from_core * quarter + n, LANES), wide)
                terms = jnp.dot(left, ref[:, n : n + wide], preferred_element_type=F32)
                for i, to_ref in enumerate((same_ref, other_ref)):
                    part = terms[i * tile // 2 : (i + 1) * tile // 2] + base_ref[rows[i], cols]
                    to_ref[:, cols] = part.astype(BF16)

    @pl.when(jnp.logical_not(match))
    def _():
        same_ref[...] = jnp.zeros(same_ref.shape, BF16)
        other_ref[...] = jnp.zeros(other_ref.shape, BF16)


def down_stay_kernel(labels_ref, place_ref, in_ref, hid_ref, mid_ref, wd_ref, sum_ref, after_ref, here_ref, there_ref, out_ref):
    tile, quarter = mid_ref.shape[0] // 2, here_ref.shape[1]
    ctx_here, section, low, core = place_ref[0], place_ref[1], place_ref[2], place_ref[3]
    match = labels_ref[0, ctx_here * 2 + section] == section
    own = halves_of(place_ref, tile)[0]
    rows = pl.ds(pl.multiple_of(own.start + tile, own.size), own.size)

    @pl.when(match)
    def _():
        arrived = in_ref[tile:, :]

        def base(cols):
            return jnp.dot(hid_ref[rows, :], wd_ref[:, cols], preferred_element_type=F32) + mid_ref[rows, cols]

        for from_core, ref in ((core, here_ref), (1 - core, there_ref)):
            for n in range(0, quarter, WIDE):
                wide = min(WIDE, quarter - n)
                cols = pl.ds(pl.multiple_of((2 * low + from_core) * quarter + n, LANES), wide)
                terms = jnp.dot(arrived, ref[:, n : n + wide], preferred_element_type=F32)
                out_ref[:, cols] = terms + base(cols)
        for n in range(0, 2 * quarter, WIDE):
            cols = pl.ds(pl.multiple_of((1 - low) * 2 * quarter + n, LANES), WIDE)
            out_ref[:, cols] = sum_ref[:, n : n + WIDE].astype(F32) + base(cols)

    @pl.when(jnp.logical_not(match))
    def _():
        out_ref[...] = jnp.zeros(out_ref.shape, F32)


def last_sum_kernel(place_ref, staying_ref, same_ref, other_ref, out_ref):
    half = same_ref.shape[1]
    low = place_ref[2]
    for at, ref in ((low, same_ref), (1 - low, other_ref)):
        for n in range(0, half, WIDE):
            cols = pl.ds(pl.multiple_of(at * half + n, LANES), WIDE)
            out_ref[:, cols] = (staying_ref[:, cols] + ref[:, n : n + WIDE].astype(F32)).astype(BF16)


SMEM = pl.BlockSpec(memory_space=pltpu.SMEM)
HBM = pl.BlockSpec(memory_space=pltpu.HBM)
VMEM = pl.BlockSpec(memory_space=pltpu.VMEM)
ANY = pl.BlockSpec(memory_space=pl.ANY)


def params(mib):
    return pltpu.CompilerParams(vmem_limit_bytes=mib * 1024 * 1024)


def stay(array):
    return pltpu.with_memory_space_constraint(array, pltpu.HBM)


def cost(flops, moved, powers=0):
    return pl.CostEstimate(flops=flops, bytes_accessed=moved, transcendentals=powers)


def w_down_quarter(place, wd):
    units, width = wd.shape
    return pl.pallas_call(
        quarter_kernel,
        out_shape=jax.ShapeDtypeStruct((units, width // 4), BF16),
        in_specs=[SMEM, HBM],
        out_specs=VMEM,
        scratch_shapes=[pltpu.SemaphoreType.DMA(())],
        compiler_params=params(8),
        cost_estimate=cost(units, units * width),
    )(place, wd)


def near_attention(split, labels, mask, place, queries, own_key, own_value, key, value):
    shard, width = queries.shape
    blocks = shard // BLOCK
    piece_rows, kv_width = key.shape
    rows = width // (KV_HEADS * HEAD_DIM) * BLOCK
    count = 2 * piece_rows
    shape = jax.ShapeDtypeStruct
    state = shape((KV_HEADS, rows, LANES), F32)
    outs = [state, state, state, shape((BLOCK, width), BF16)] * blocks
    made = pl.pallas_call(
        functools.partial(near_kernel, split),
        out_shape=outs,
        in_specs=[SMEM, SMEM, SMEM, HBM, HBM, HBM, VMEM, VMEM],
        out_specs=[VMEM] * len(outs),
        scratch_shapes=[
            pltpu.VMEM((piece_rows, kv_width), BF16),
            pltpu.VMEM((piece_rows, kv_width), BF16),
            pltpu.VMEM((blocks, 2, piece_rows, BLOCK), BF16),
            pltpu.VMEM((2, rows, count), F32),
            pltpu.SemaphoreType.DMA((blocks,)),
            pltpu.SemaphoreType.DMA((2,)),
        ],
        compiler_params=params(16),
        cost_estimate=cost(40 * shard * width * count, 2 * shard * width, shard * width // HEAD_DIM * count),
    )(labels, mask, place, queries, own_key, own_value, key, value)
    return [list(made[4 * i : 4 * i + 4]) for i in range(blocks)]


def far_attention(split, pieces, labels, mask, place, residual, gains, states, keys, values, wg, wu, wd):
    tile, width = states[0][3].shape
    piece_rows = keys[0].shape[0]
    rows = width // (KV_HEADS * HEAD_DIM) * BLOCK
    count = piece_rows * len(pieces)
    units = wg.shape[0]
    up_at = -(-units // LANES) * LANES
    taken = tile * len(states)
    shape = jax.ShapeDtypeStruct
    if split:
        outs = [shape((tile + tile // 2, units), BF16), shape((taken, units), BF16)]
        outs += [shape((taken, width), F32), shape(wd.shape, BF16), shape((tile // 2, width // 2), BF16)]
    else:
        outs = [shape((taken, width), F32)]
    return pl.pallas_call(
        functools.partial(far_kernel, split, pieces),
        out_shape=outs,
        in_specs=[SMEM, SMEM, SMEM, HBM, VMEM] + [VMEM] * (4 * len(states) + 2 * len(pieces)) + [HBM] * 3,
        out_specs=[VMEM] * len(outs),
        scratch_shapes=[
            pltpu.VMEM((taken, width), BF16),
            pltpu.VMEM((up_at + units, width), BF16),
            pltpu.VMEM((16, LANES) if split else wd.shape, BF16),
            pltpu.VMEM((len(pieces), piece_rows, BLOCK), BF16),
            pltpu.VMEM((2, rows, count), F32),
            pltpu.VMEM((taken, width), BF16),
            pltpu.VMEM((taken, width), BF16),
            pltpu.VMEM((taken, units), BF16),
            pltpu.SemaphoreType.DMA((len(states),)),
            pltpu.SemaphoreType.DMA((3,)),
        ],
        compiler_params=params(28),
        cost_estimate=cost(taken * width, width, taken),
    )(
        labels, mask, place, residual, gains, *[array for state in states for array in state],
        *keys, *values, wg, wu, wd,
    )


TOKEN = jax.ShapeDtypeStruct((8, LANES), F32)


def down_own(labels, place, hid, mid, wd):
    rows, width = mid.shape
    return pl.pallas_call(
        down_own_kernel,
        out_shape=jax.ShapeDtypeStruct((rows // 2, width // 2), F32),
        in_specs=[SMEM, SMEM] + [VMEM] * 3,
        out_specs=VMEM,
        compiler_params=params(16),
        cost_estimate=cost(40 * rows * wd.size, wd.size),
    )(labels, place, hid, mid, wd)


def down_leave(labels, place, arrived, base, here, there):
    tile, half_width = base.shape
    half = jax.ShapeDtypeStruct((tile // 2, half_width), BF16)
    return pl.pallas_call(
        down_leave_kernel,
        out_shape=[half, half, TOKEN],
        in_specs=[SMEM, SMEM] + [VMEM] * 4,
        out_specs=[VMEM] * 3,
        compiler_params=params(16),
        cost_estimate=cost(tile, tile),
    )(labels, place, arrived, base, here, there)


def down_stay(labels, place, arrived, hid, mid, wd, summed, after, here, there):
    rows, width = mid.shape
    return pl.pallas_call(
        down_stay_kernel,
        out_shape=jax.ShapeDtypeStruct((rows // 4, width), F32),
        in_specs=[SMEM, SMEM] + [VMEM] * 5 + [ANY] + [VMEM] * 2,
        out_specs=VMEM,
        compiler_params=params(16),
        cost_estimate=cost(40 * rows * wd.size, wd.size),
    )(labels, place, arrived, hid, mid, wd, summed, after, here, there)


def last_sum(place, staying, same, other):
    return pl.pallas_call(
        last_sum_kernel,
        out_shape=jax.ShapeDtypeStruct(staying.shape, BF16),
        in_specs=[SMEM] + [VMEM] * 3,
        out_specs=VMEM,
        compiler_params=params(8),
        cost_estimate=cost(staying.size, staying.size),
    )(place, staying, same, other)


def xor_pairs(count, bits):
    return [(i, i ^ bits) for i in range(count)]


def per_device(queries, keys, values, residual, labels, block_mask, gains, w_gate, w_up, w_down):
    shard, width = queries.shape[1:]
    exp_count = lax.axis_size("exp")
    exp_here = lax.axis_index("exp")
    ctx_count = lax.axis_size("ctx")
    ctx_here = lax.axis_index("ctx")
    half = exp_count // 2
    split = exp_count == 4 and shard == 2 * BLOCK and ctx_count == 4
    section = exp_here // half
    low = exp_here % 2 if split else jnp.zeros_like(exp_here)
    core = ctx_here % 2
    first = exp_here % half == 0
    place = jnp.stack([value.astype(jnp.int32) for value in (ctx_here, section, low, core, first)])
    labels, block_mask, gains = stay(labels), stay(block_mask), stay(gains)
    own_q, own_res = stay(queries[0]), stay(residual[0])

    held = {0: (keys[0], values[0])}

    def spread(bits):
        pairs = xor_pairs(ctx_count, bits)
        for at, (k, v) in list(held.items()):
            held[at ^ bits] = (lax.ppermute(k, "ctx", pairs), lax.ppermute(v, "ctx", pairs))

    def swap(array):
        return lax.ppermute(array, "ctx", xor_pairs(ctx_count, 1))

    bits = ctx_count // 2
    while bits > 1:
        spread(bits)
        bits //= 2
    held[1] = (swap(keys[0]), swap(values[0]))
    z_pairs = xor_pairs(exp_count, 1)
    if split:
        here = lax.ppermute(w_down_quarter(place, stay(w_down)), "exp", z_pairs)
    states = near_attention(
        split, labels, block_mask, place, own_q, stay(keys[0]), stay(values[0]), *held[1]
    )
    for at in range(2, ctx_count, 2):
        k, v = held[at]
        k, v, states[0][0] = lax.optimization_barrier((k, v, states[0][0]))
        held[at] = (k, v)
        held[at + 1] = (swap(k), swap(v))
    far = range(2, ctx_count)
    far_keys, far_values = [held[c][0] for c in far], [held[c][1] for c in far]
    weights = (far_keys, far_values, stay(w_gate.T), stay(w_up.T), stay(w_down))
    shared = (labels, block_mask, place, own_res, gains)
    made = far_attention(split, far, *shared, states, *weights)
    if not split:
        return lax.psum_scatter(made[0][None], "exp", scatter_dimension=1, tiled=True).astype(BF16)

    send, hid, mid, own_wd, sent = made
    here, send = lax.optimization_barrier((here, send))
    there = swap(here)
    arrived = lax.ppermute(send, "exp", z_pairs)
    base = down_own(labels, place, hid, mid, own_wd)
    arrived, sent, base = lax.optimization_barrier((arrived, sent, base))
    same, other, token = down_leave(labels, place, arrived, base, here, there)
    same, other = (
        lax.ppermute(part, "exp", xor_pairs(exp_count, bits)) for part, bits in ((same, 2), (other, 3))
    )
    summed = lax.ppermute(sent, "exp", z_pairs)
    staying = down_stay(labels, place, arrived, hid, mid, own_wd, summed, token, here, there)
    return last_sum(place, staying, same, other)[None]


def solution(mesh):
    placed = (
        P("dp", "ctx", None),
        P("dp", "ctx", None),
        P("dp", "ctx", None),
        P("dp", "ctx", None),
        P("dp", None),
        P("dp", None, None),
        P(),
        P(None, "exp"),
        P(None, "exp"),
        P("exp", None),
    )
    return jax.shard_map(
        per_device,
        mesh=mesh,
        in_specs=placed,
        out_specs=P("dp", ("ctx", "exp"), None),
        check_vma=False,
    )
```

```python
import functools

import jax
import jax.numpy as jnp
from jax import lax
from jax.experimental import pallas as pl
from jax.experimental.pallas import tpu as pltpu
from jax.sharding import PartitionSpec as P

KV_HEADS = 4
HEAD_DIM = 128
BLOCK = 128
LANES = 128
MASKED = -1e30
EXP2_SCALE = 1.4426950408889634 / (HEAD_DIM**0.5)
BF16 = jnp.bfloat16
F32 = jnp.float32
OVER_LAST = (((1,), (1,)), ((), ()))
WIDE = 256


def fill_bias(bias_ref, mask_ref, labels_ref, here, shards):
    key_in = lax.broadcasted_iota(jnp.int32, (BLOCK, BLOCK), 0)
    query_in = lax.broadcasted_iota(jnp.int32, (BLOCK, BLOCK), 1)
    later = (key_in > query_in).astype(jnp.int32)
    piece_blocks = bias_ref.shape[1] // BLOCK
    any_open = jnp.int32(0)
    for c, shard_of in enumerate(shards):
        for b in range(piece_blocks):
            other = shard_of * piece_blocks + b
            is_open = mask_ref[0, here, other]
            any_open = any_open | is_open
            closed = jnp.where(other == here, 1 - labels_ref[0, here], 0) * later
            closed = jnp.where(is_open == 1, closed, 1)
            bias_ref[c, b * BLOCK : (b + 1) * BLOCK, :] = jnp.where(closed == 1, MASKED, 0.0).astype(BF16)
    return any_open


def attend(q_ref, key_refs, value_refs, bias_ref, s_buf, prior, finish):
    tile, width = q_ref.shape
    group = width // (KV_HEADS * HEAD_DIM)
    rows = group * tile
    row_ids = lax.broadcasted_iota(jnp.int32, (tile, BLOCK), 0)
    col_ids = lax.broadcasted_iota(jnp.int32, (tile, BLOCK), 1)
    picks = jnp.where(row_ids == col_ids, 1.0, 0.0).astype(BF16)
    ones = jnp.ones((key_refs[0].shape[0], HEAD_DIM), BF16)
    limits = {}

    def score(g):
        q_all = jnp.concatenate(
            [
                jnp.concatenate([q_ref[:, (g * group + h) * HEAD_DIM : (g * group + h + 1) * HEAD_DIM], picks], axis=1)
                for h in range(group)
            ],
            axis=0,
        )
        lanes = slice(g * HEAD_DIM, (g + 1) * HEAD_DIM)
        k_all = jnp.concatenate(
            [jnp.concatenate([ref[:, lanes], bias_ref[c]], axis=1) for c, ref in enumerate(key_refs)], axis=0
        )
        s = lax.dot_general(q_all, k_all, OVER_LAST, preferred_element_type=F32)
        s_buf[g % 2] = s
        top = functools.reduce(jnp.maximum, [s[:, n : n + LANES] for n in range(0, s.shape[1], LANES)])
        top = jnp.broadcast_to(jnp.max(top, axis=1, keepdims=True), (rows, LANES))
        if prior is not None:
            top = jnp.maximum(top, prior(g)[2])
        limits[g] = top

    def mix(g):
        lanes = slice(g * HEAD_DIM, (g + 1) * HEAD_DIM)
        shift = limits[g] * EXP2_SCALE
        soft = jnp.concatenate(
            [
                jnp.exp2(s_buf[g % 2, :, n : n + LANES] * EXP2_SCALE - shift).astype(BF16)
                for n in range(0, s_buf.shape[2], LANES)
            ],
            axis=1,
        )
        v_all = jnp.concatenate([jnp.concatenate([ref[:, lanes], ones], axis=1) for ref in value_refs], axis=0)
        mixed = jnp.dot(soft, v_all, preferred_element_type=F32)
        sums, totals = mixed[:, :HEAD_DIM], mixed[:, HEAD_DIM:]
        if prior is not None:
            before = prior(g)
            factor = jnp.exp2((before[2] - limits[g]) * EXP2_SCALE)
            sums = sums + before[0] * factor
            totals = totals + before[1] * factor
        finish(g, sums, totals, limits[g])

    score(0)
    for g in range(KV_HEADS):
        if g + 1 < KV_HEADS:
            score(g + 1)
        mix(g)


def quarter_kernel(place_ref, wd_hbm, out_ref, sem):
    low, core = place_ref[2], place_ref[3]
    width = wd_hbm.shape[1]
    cols = pl.ds(pl.multiple_of((1 - low) * (width // 2) + core * (width // 4), LANES), width // 4)
    copy = pltpu.make_async_copy(wd_hbm.at[:, cols], out_ref, sem)
    copy.start()
    copy.wait()


def near_kernel(split, labels_ref, mask_ref, place_ref, q_hbm, k_hbm, v_hbm, k_ref, v_ref, *rest):
    k_buf, v_buf, bias_buf, s_buf, sem, kv_sem = rest[-6:]
    blocks = len(rest[:-6]) // 4
    outs = [rest[4 * i : 4 * i + 4] for i in range(blocks)]
    tile = outs[0][3].shape[0]
    ctx_here, section = place_ref[0], place_ref[1]
    order = [1 - section, section] if split else list(range(blocks))

    loads = [
        pltpu.make_async_copy(q_hbm.at[pl.ds(pl.multiple_of(t * tile, tile), tile)], outs[i][3], sem.at[i])
        for i, t in enumerate(order)
    ]
    loads.append(pltpu.make_async_copy(k_hbm, k_buf, kv_sem.at[0]))
    loads.append(pltpu.make_async_copy(v_hbm, v_buf, kv_sem.at[1]))
    for copy in loads:
        copy.start()
    for i, t in enumerate(order):
        fill_bias(bias_buf.at[i], mask_ref, labels_ref, ctx_here * blocks + t, [ctx_here, ctx_here ^ 1])
    for copy in loads:
        copy.wait()

    for i, t in enumerate(order):
        sums_ref, totals_ref, limits_ref, q_ref = outs[i]

        @pl.when(labels_ref[0, ctx_here * blocks + t] == section)
        def _():
            def finish(g, sums, totals, limit):
                sums_ref[g] = sums
                totals_ref[g] = totals
                limits_ref[g] = limit

            attend(q_ref, [k_buf, k_ref], [v_buf, v_ref], bias_buf.at[i], s_buf, None, finish)


def attend_far(match, here, pieces, refs, att_ref, bias_buf, s_buf):
    labels_ref, mask_ref, place_ref, key_refs, value_refs, sums_ref, totals_ref, limits_ref, q_ref = refs
    tile, width = att_ref.shape
    group = width // (KV_HEADS * HEAD_DIM)
    opened = fill_bias(bias_buf, mask_ref, labels_ref, here, [place_ref[0] ^ c for c in pieces])

    def finish(g, sums, totals, _):
        attended = (sums / totals).astype(BF16)
        for h in range(group):
            at = (g * group + h) * HEAD_DIM
            att_ref[:, at : at + HEAD_DIM] = attended[h * tile : (h + 1) * tile]

    def prior(g):
        return sums_ref[g], totals_ref[g], limits_ref[g]

    @pl.when(match & (opened > 0))
    def _():
        attend(q_ref, key_refs, value_refs, bias_buf, s_buf, prior, finish)

    @pl.when(match & (opened == 0))
    def _():
        for g in range(KV_HEADS):
            finish(g, sums_ref[g], totals_ref[g], None)


def norm_block(gains_ref, section, first_row, tile, mid_of, norm_buf):
    gain = gains_ref[pl.ds(section, 1), :]
    step = 16

    def norm_rows(j, carry):
        rows = pl.ds(pl.multiple_of(first_row + j * step, step), step)
        mid = mid_of(rows, slice(None))
        factor = lax.rsqrt(jnp.mean(mid * mid, axis=-1, keepdims=True) + 1e-05)
        norm_buf[rows, :] = (mid * factor * gain).astype(BF16)
        return carry

    lax.fori_loop(0, tile // step, norm_rows, 0)


def hidden_of(norm_buf, w_ref, units):
    up_at = w_ref.shape[0] - units
    both = lax.dot_general(norm_buf[...], w_ref[...], OVER_LAST, preferred_element_type=F32)
    gate, upper = both[:, :units], both[:, up_at : up_at + units]
    return (gate * upper / (1.0 + jnp.exp(-gate))).astype(BF16)


def halves_of(place_ref, tile):
    half = tile // 2
    low = place_ref[2]
    own = pl.ds(pl.multiple_of(low * half, half), half)
    return own, pl.ds(pl.multiple_of(half - low * half, half), half)


def far_kernel(split, pieces, labels_ref, mask_ref, place_ref, res_hbm, gains_ref, *rest):
    tile, width = rest[3].shape
    blocks = res_hbm.shape[0] // tile
    state_refs, rest = rest[: 4 * blocks], rest[4 * blocks :]
    count = len(pieces)
    key_refs, value_refs = rest[:count], rest[count : 2 * count]
    wg_hbm, wu_hbm, wd_hbm = rest[2 * count : 2 * count + 3]
    out_refs = rest[2 * count + 3 : -10]
    res_buf, w_buf, wd_buf, bias_buf, s_buf, att_buf, norm_buf, hid_buf, sem, w_sem = rest[-10:]
    if split:
        send_ref, hid_ref, mid_ref, wd_buf, sent_ref = out_refs
    units = wg_hbm.shape[0]
    ctx_here, section, first = place_ref[0], place_ref[1], place_ref[4]
    chosen = [1 - section, section] if split else list(range(blocks))
    refs = (labels_ref, mask_ref, place_ref, key_refs, value_refs)

    loads = []
    for i, t in enumerate(chosen):
        rows = pl.ds(pl.multiple_of(t * tile, tile), tile)
        loads.append(pltpu.make_async_copy(res_hbm.at[rows], res_buf.at[pl.ds(i * tile, tile)], sem.at[i]))
    loads.append(pltpu.make_async_copy(wg_hbm, w_buf.at[pl.ds(0, units)], w_sem.at[0]))
    loads.append(pltpu.make_async_copy(wu_hbm, w_buf.at[pl.ds(w_buf.shape[0] - units, units)], w_sem.at[1]))
    later = pltpu.make_async_copy(wd_hbm, wd_buf, w_sem.at[2])
    for copy in loads:
        copy.start()
    later.start()

    matches = [labels_ref[0, ctx_here * blocks + t] == section for t in chosen]
    for i, t in enumerate(chosen):
        span = pl.ds(i * tile, tile)
        block_refs = (*refs, *state_refs[4 * i : 4 * i + 4])
        attend_far(matches[i], ctx_here * blocks + t, pieces, block_refs, att_buf.at[span], bias_buf, s_buf)

        @pl.when(jnp.logical_not(matches[i]))
        def _():
            norm_buf[span, :] = jnp.zeros((tile, width), BF16)

    for copy in loads:
        copy.wait()

    def mid_of(rows, cols):
        mid = res_buf[rows, cols].astype(F32) + att_buf[rows, cols].astype(F32)
        if split:
            mid_ref[rows, cols] = mid
        return mid

    for i in range(len(chosen)):

        @pl.when(matches[i])
        def _():
            norm_block(gains_ref, section, i * tile, tile, mid_of, norm_buf)

    later.wait()

    @pl.when(functools.reduce(jnp.logical_or, matches))
    def _():
        hid_buf[...] = hidden_of(norm_buf, w_buf, units)
        if split:
            other = halves_of(place_ref, tile)[1]
            other = pl.ds(pl.multiple_of(other.start + tile, other.size), other.size)
            hid_ref[...] = hid_buf[...]
            send_ref[:tile, :] = hid_buf[:tile, :]
            send_ref[tile:, :] = hid_buf[other, :]

            @pl.when(matches[1])
            def _():
                for n in range(0, width // 2, WIDE):
                    cols = pl.ds(pl.multiple_of(place_ref[2] * (width // 2) + n, LANES), WIDE)
                    terms = jnp.dot(hid_buf[other, :], wd_buf[:, cols], preferred_element_type=F32)
                    sent_ref[:, n : n + WIDE] = terms.astype(BF16)

        else:
            for n in range(0, width, WIDE):
                cols = slice(n, n + WIDE)
                terms = jnp.dot(hid_buf[...], wd_buf[:, cols], preferred_element_type=F32)
                for i in range(blocks):
                    span = slice(i * tile, (i + 1) * tile)
                    kept = terms[span] + mid_of(span, cols) * first.astype(F32)
                    out_refs[0][span, cols] = jnp.where(matches[i], kept, 0.0)

    if not split:

        @pl.when(jnp.logical_not(functools.reduce(jnp.logical_or, matches)))
        def _():
            out_refs[0][...] = jnp.zeros(out_refs[0].shape, F32)


def down_own_kernel(labels_ref, place_ref, hid_ref, mid_ref, wd_ref, out_ref):
    tile, half = out_ref.shape
    ctx_here, section, low = place_ref[0], place_ref[1], place_ref[2]

    @pl.when(labels_ref[0, ctx_here * 2 + 1 - section] == section)
    def _():
        for n in range(0, half, WIDE):
            cols = pl.ds(pl.multiple_of(low * half + n, LANES), WIDE)
            terms = jnp.dot(hid_ref[:tile, :], wd_ref[:, cols], preferred_element_type=F32)
            out_ref[:, n : n + WIDE] = terms + mid_ref[:tile, cols]


def down_leave_kernel(labels_ref, place_ref, in_ref, base_ref, here_ref, there_ref, same_ref, other_ref, token_ref):
    tile, quarter = base_ref.shape[0], here_ref.shape[1]
    ctx_here, section, core = place_ref[0], place_ref[1], place_ref[3]
    match = labels_ref[0, ctx_here * 2 + 1 - section] == section
    token_ref[...] = jnp.zeros(token_ref.shape, F32)
    rows = halves_of(place_ref, tile)

    @pl.when(match)
    def _():
        left = jnp.concatenate([in_ref[span, :] for span in rows], axis=0)
        for from_core, ref in ((core, here_ref), (1 - core, there_ref)):
            for n in range(0, quarter, WIDE):
                wide = min(WIDE, quarter - n)
                cols = pl.ds(pl.multiple_of(from_core * quarter + n, LANES), wide)
                terms = jnp.dot(left, ref[:, n : n + wide], preferred_element_type=F32)
                for i, to_ref in enumerate((same_ref, other_ref)):
                    part = terms[i * tile // 2 : (i + 1) * tile // 2] + base_ref[rows[i], cols]
                    to_ref[:, cols] = part.astype(BF16)

    @pl.when(jnp.logical_not(match))
    def _():
        same_ref[...] = jnp.zeros(same_ref.shape, BF16)
        other_ref[...] = jnp.zeros(other_ref.shape, BF16)


def down_stay_kernel(labels_ref, place_ref, in_ref, hid_ref, mid_ref, wd_ref, sum_ref, after_ref, here_ref, there_ref, out_ref):
    tile, quarter = mid_ref.shape[0] // 2, here_ref.shape[1]
    ctx_here, section, low, core = place_ref[0], place_ref[1], place_ref[2], place_ref[3]
    match = labels_ref[0, ctx_here * 2 + section] == section
    own = halves_of(place_ref, tile)[0]
    rows = pl.ds(pl.multiple_of(own.start + tile, own.size), own.size)

    @pl.when(match)
    def _():
        arrived = in_ref[tile:, :]

        def base(cols):
            return jnp.dot(hid_ref[rows, :], wd_ref[:, cols], preferred_element_type=F32) + mid_ref[rows, cols]

        for from_core, ref in ((core, here_ref), (1 - core, there_ref)):
            for n in range(0, quarter, WIDE):
                wide = min(WIDE, quarter - n)
                cols = pl.ds(pl.multiple_of((2 * low + from_core) * quarter + n, LANES), wide)
                terms = jnp.dot(arrived, ref[:, n : n + wide], preferred_element_type=F32)
                out_ref[:, cols] = terms + base(cols)
        for n in range(0, 2 * quarter, WIDE):
            cols = pl.ds(pl.multiple_of((1 - low) * 2 * quarter + n, LANES), WIDE)
            out_ref[:, cols] = sum_ref[:, n : n + WIDE].astype(F32) + base(cols)

    @pl.when(jnp.logical_not(match))
    def _():
        out_ref[...] = jnp.zeros(out_ref.shape, F32)


def last_sum_kernel(place_ref, staying_ref, same_ref, other_ref, out_ref):
    half = same_ref.shape[1]
    low = place_ref[2]
    for at, ref in ((low, same_ref), (1 - low, other_ref)):
        for n in range(0, half, WIDE):
            cols = pl.ds(pl.multiple_of(at * half + n, LANES), WIDE)
            out_ref[:, cols] = (staying_ref[:, cols] + ref[:, n : n + WIDE].astype(F32)).astype(BF16)


SMEM = pl.BlockSpec(memory_space=pltpu.SMEM)
HBM = pl.BlockSpec(memory_space=pltpu.HBM)
VMEM = pl.BlockSpec(memory_space=pltpu.VMEM)
ANY = pl.BlockSpec(memory_space=pl.ANY)


def params(mib):
    return pltpu.CompilerParams(vmem_limit_bytes=mib * 1024 * 1024)


def stay(array):
    return pltpu.with_memory_space_constraint(array, pltpu.HBM)


def cost(flops, moved, powers=0):
    return pl.CostEstimate(flops=flops, bytes_accessed=moved, transcendentals=powers)


def w_down_quarter(place, wd):
    units, width = wd.shape
    return pl.pallas_call(
        quarter_kernel,
        out_shape=jax.ShapeDtypeStruct((units, width // 4), BF16),
        in_specs=[SMEM, HBM],
        out_specs=VMEM,
        scratch_shapes=[pltpu.SemaphoreType.DMA(())],
        compiler_params=params(8),
        cost_estimate=cost(units, units * width),
    )(place, wd)


def near_attention(split, labels, mask, place, queries, own_key, own_value, key, value):
    shard, width = queries.shape
    blocks = shard // BLOCK
    piece_rows, kv_width = key.shape
    rows = width // (KV_HEADS * HEAD_DIM) * BLOCK
    count = 2 * piece_rows
    shape = jax.ShapeDtypeStruct
    state = shape((KV_HEADS, rows, LANES), F32)
    outs = [state, state, state, shape((BLOCK, width), BF16)] * blocks
    made = pl.pallas_call(
        functools.partial(near_kernel, split),
        out_shape=outs,
        in_specs=[SMEM, SMEM, SMEM, HBM, HBM, HBM, VMEM, VMEM],
        out_specs=[VMEM] * len(outs),
        scratch_shapes=[
            pltpu.VMEM((piece_rows, kv_width), BF16),
            pltpu.VMEM((piece_rows, kv_width), BF16),
            pltpu.VMEM((blocks, 2, piece_rows, BLOCK), BF16),
            pltpu.VMEM((2, rows, count), F32),
            pltpu.SemaphoreType.DMA((blocks,)),
            pltpu.SemaphoreType.DMA((2,)),
        ],
        compiler_params=params(16),
        cost_estimate=cost(40 * shard * width * count, 2 * shard * width, shard * width // HEAD_DIM * count),
    )(labels, mask, place, queries, own_key, own_value, key, value)
    return [list(made[4 * i : 4 * i + 4]) for i in range(blocks)]


def far_attention(split, pieces, labels, mask, place, residual, gains, states, keys, values, wg, wu, wd):
    tile, width = states[0][3].shape
    piece_rows = keys[0].shape[0]
    rows = width // (KV_HEADS * HEAD_DIM) * BLOCK
    count = piece_rows * len(pieces)
    units = wg.shape[0]
    up_at = -(-units // LANES) * LANES
    taken = tile * len(states)
    shape = jax.ShapeDtypeStruct
    if split:
        outs = [shape((tile + tile // 2, units), BF16), shape((taken, units), BF16)]
        outs += [shape((taken, width), F32), shape(wd.shape, BF16), shape((tile // 2, width // 2), BF16)]
    else:
        outs = [shape((taken, width), F32)]
    return pl.pallas_call(
        functools.partial(far_kernel, split, pieces),
        out_shape=outs,
        in_specs=[SMEM, SMEM, SMEM, HBM, VMEM] + [VMEM] * (4 * len(states) + 2 * len(pieces)) + [HBM] * 3,
        out_specs=[VMEM] * len(outs),
        scratch_shapes=[
            pltpu.VMEM((taken, width), BF16),
            pltpu.VMEM((up_at + units, width), BF16),
            pltpu.VMEM((16, LANES) if split else wd.shape, BF16),
            pltpu.VMEM((len(pieces), piece_rows, BLOCK), BF16),
            pltpu.VMEM((2, rows, count), F32),
            pltpu.VMEM((taken, width), BF16),
            pltpu.VMEM((taken, width), BF16),
            pltpu.VMEM((taken, units), BF16),
            pltpu.SemaphoreType.DMA((len(states),)),
            pltpu.SemaphoreType.DMA((3,)),
        ],
        compiler_params=params(28),
        cost_estimate=cost(taken * width, width, taken),
    )(
        labels, mask, place, residual, gains, *[array for state in states for array in state],
        *keys, *values, wg, wu, wd,
    )


TOKEN = jax.ShapeDtypeStruct((8, LANES), F32)


def down_own(labels, place, hid, mid, wd):
    rows, width = mid.shape
    return pl.pallas_call(
        down_own_kernel,
        out_shape=jax.ShapeDtypeStruct((rows // 2, width // 2), F32),
        in_specs=[SMEM, SMEM] + [VMEM] * 3,
        out_specs=VMEM,
        compiler_params=params(16),
        cost_estimate=cost(40 * rows * wd.size, wd.size),
    )(labels, place, hid, mid, wd)


def down_leave(labels, place, arrived, base, here, there):
    tile, half_width = base.shape
    half = jax.ShapeDtypeStruct((tile // 2, half_width), BF16)
    return pl.pallas_call(
        down_leave_kernel,
        out_shape=[half, half, TOKEN],
        in_specs=[SMEM, SMEM] + [VMEM] * 4,
        out_specs=[VMEM] * 3,
        compiler_params=params(16),
        cost_estimate=cost(tile, tile),
    )(labels, place, arrived, base, here, there)


def down_stay(labels, place, arrived, hid, mid, wd, summed, after, here, there):
    rows, width = mid.shape
    return pl.pallas_call(
        down_stay_kernel,
        out_shape=jax.ShapeDtypeStruct((rows // 4, width), F32),
        in_specs=[SMEM, SMEM] + [VMEM] * 5 + [ANY] + [VMEM] * 2,
        out_specs=VMEM,
        compiler_params=params(16),
        cost_estimate=cost(40 * rows * wd.size, wd.size),
    )(labels, place, arrived, hid, mid, wd, summed, after, here, there)


def last_sum(place, staying, same, other):
    return pl.pallas_call(
        last_sum_kernel,
        out_shape=jax.ShapeDtypeStruct(staying.shape, BF16),
        in_specs=[SMEM] + [VMEM] * 3,
        out_specs=VMEM,
        compiler_params=params(8),
        cost_estimate=cost(staying.size, staying.size),
    )(place, staying, same, other)


def xor_pairs(count, bits):
    return [(i, i ^ bits) for i in range(count)]


def per_device(queries, keys, values, residual, labels, block_mask, gains, w_gate, w_up, w_down):
    shard, width = queries.shape[1:]
    exp_count = lax.axis_size("exp")
    exp_here = lax.axis_index("exp")
    ctx_count = lax.axis_size("ctx")
    ctx_here = lax.axis_index("ctx")
    half = exp_count // 2
    split = exp_count == 4 and shard == 2 * BLOCK and ctx_count == 4
    section = exp_here // half
    low = exp_here % 2 if split else jnp.zeros_like(exp_here)
    core = ctx_here % 2
    first = exp_here % half == 0
    place = jnp.stack([value.astype(jnp.int32) for value in (ctx_here, section, low, core, first)])
    labels, block_mask, gains = stay(labels), stay(block_mask), stay(gains)
    own_q, own_res = stay(queries[0]), stay(residual[0])

    held = {0: (keys[0], values[0])}

    def spread(bits):
        pairs = xor_pairs(ctx_count, bits)
        for at, (k, v) in list(held.items()):
            held[at ^ bits] = (lax.ppermute(k, "ctx", pairs), lax.ppermute(v, "ctx", pairs))

    def swap(array):
        return lax.ppermute(array, "ctx", xor_pairs(ctx_count, 1))

    bits = ctx_count // 2
    while bits > 1:
        spread(bits)
        bits //= 2
    held[1] = (swap(keys[0]), swap(values[0]))
    z_pairs = xor_pairs(exp_count, 1)
    if split:
        here = lax.ppermute(w_down_quarter(place, stay(w_down)), "exp", z_pairs)
    states = near_attention(
        split, labels, block_mask, place, own_q, stay(keys[0]), stay(values[0]), *held[1]
    )
    for at in range(2, ctx_count, 2):
        k, v = held[at]
        k, v, states[0][0] = lax.optimization_barrier((k, v, states[0][0]))
        held[at] = (k, v)
        held[at + 1] = (swap(k), swap(v))
    far = range(2, ctx_count)
    far_keys, far_values = [held[c][0] for c in far], [held[c][1] for c in far]
    weights = (far_keys, far_values, stay(w_gate.T), stay(w_up.T), stay(w_down))
    shared = (labels, block_mask, place, own_res, gains)
    made = far_attention(split, far, *shared, states, *weights)
    if not split:
        return lax.psum_scatter(made[0][None], "exp", scatter_dimension=1, tiled=True).astype(BF16)

    send, hid, mid, own_wd, sent = made
    here, send = lax.optimization_barrier((here, send))
    there = swap(here)
    arrived = lax.ppermute(send, "exp", z_pairs)
    base = down_own(labels, place, hid, mid, own_wd)
    sent, there = lax.optimization_barrier((sent, there))
    same, other, token = down_leave(labels, place, arrived, base, here, there)
    same, other = (
        lax.ppermute(part, "exp", xor_pairs(exp_count, bits)) for part, bits in ((same, 2), (other, 3))
    )
    summed = lax.ppermute(sent, "exp", z_pairs)
    staying = down_stay(labels, place, arrived, hid, mid, own_wd, summed, token, here, there)
    return last_sum(place, staying, same, other)[None]


def solution(mesh):
    placed = (
        P("dp", "ctx", None),
        P("dp", "ctx", None),
        P("dp", "ctx", None),
        P("dp", "ctx", None),
        P("dp", None),
        P("dp", None, None),
        P(),
        P(None, "exp"),
        P(None, "exp"),
        P("exp", None),
    )
    return jax.shard_map(
        per_device,
        mesh=mesh,
        in_specs=placed,
        out_specs=P("dp", ("ctx", "exp"), None),
        check_vma=False,
    )
```

```python
import functools

import jax
import jax.numpy as jnp
from jax import lax
from jax.experimental import pallas as pl
from jax.experimental.pallas import tpu as pltpu
from jax.sharding import PartitionSpec as P

KV_HEADS = 4
HEAD_DIM = 128
BLOCK = 128
LANES = 128
MASKED = -1e30
EXP2_SCALE = 1.4426950408889634 / (HEAD_DIM**0.5)
BF16 = jnp.bfloat16
F32 = jnp.float32
OVER_LAST = (((1,), (1,)), ((), ()))
WIDE = 256


def fill_bias(bias_ref, mask_ref, labels_ref, here, shards):
    key_in = lax.broadcasted_iota(jnp.int32, (BLOCK, BLOCK), 0)
    query_in = lax.broadcasted_iota(jnp.int32, (BLOCK, BLOCK), 1)
    later = (key_in > query_in).astype(jnp.int32)
    piece_blocks = bias_ref.shape[1] // BLOCK
    any_open = jnp.int32(0)
    for c, shard_of in enumerate(shards):
        for b in range(piece_blocks):
            other = shard_of * piece_blocks + b
            is_open = mask_ref[0, here, other]
            any_open = any_open | is_open
            closed = jnp.where(other == here, 1 - labels_ref[0, here], 0) * later
            closed = jnp.where(is_open == 1, closed, 1)
            bias_ref[c, b * BLOCK : (b + 1) * BLOCK, :] = jnp.where(closed == 1, MASKED, 0.0).astype(BF16)
    return any_open


def attend(q_ref, key_refs, value_refs, bias_ref, s_buf, prior, finish):
    tile, width = q_ref.shape
    group = width // (KV_HEADS * HEAD_DIM)
    rows = group * tile
    row_ids = lax.broadcasted_iota(jnp.int32, (tile, BLOCK), 0)
    col_ids = lax.broadcasted_iota(jnp.int32, (tile, BLOCK), 1)
    picks = jnp.where(row_ids == col_ids, 1.0, 0.0).astype(BF16)
    ones = jnp.ones((key_refs[0].shape[0], HEAD_DIM), BF16)
    limits = {}

    def score(g):
        q_all = jnp.concatenate(
            [
                jnp.concatenate([q_ref[:, (g * group + h) * HEAD_DIM : (g * group + h + 1) * HEAD_DIM], picks], axis=1)
                for h in range(group)
            ],
            axis=0,
        )
        lanes = slice(g * HEAD_DIM, (g + 1) * HEAD_DIM)
        k_all = jnp.concatenate(
            [jnp.concatenate([ref[:, lanes], bias_ref[c]], axis=1) for c, ref in enumerate(key_refs)], axis=0
        )
        s = lax.dot_general(q_all, k_all, OVER_LAST, preferred_element_type=F32)
        s_buf[g % 2] = s
        top = functools.reduce(jnp.maximum, [s[:, n : n + LANES] for n in range(0, s.shape[1], LANES)])
        top = jnp.broadcast_to(jnp.max(top, axis=1, keepdims=True), (rows, LANES))
        if prior is not None:
            top = jnp.maximum(top, prior(g)[2])
        limits[g] = top

    def mix(g):
        lanes = slice(g * HEAD_DIM, (g + 1) * HEAD_DIM)
        shift = limits[g] * EXP2_SCALE
        soft = jnp.concatenate(
            [
                jnp.exp2(s_buf[g % 2, :, n : n + LANES] * EXP2_SCALE - shift).astype(BF16)
                for n in range(0, s_buf.shape[2], LANES)
            ],
            axis=1,
        )
        v_all = jnp.concatenate([jnp.concatenate([ref[:, lanes], ones], axis=1) for ref in value_refs], axis=0)
        mixed = jnp.dot(soft, v_all, preferred_element_type=F32)
        sums, totals = mixed[:, :HEAD_DIM], mixed[:, HEAD_DIM:]
        if prior is not None:
            before = prior(g)
            factor = jnp.exp2((before[2] - limits[g]) * EXP2_SCALE)
            sums = sums + before[0] * factor
            totals = totals + before[1] * factor
        finish(g, sums, totals, limits[g])

    score(0)
    for g in range(KV_HEADS):
        if g + 1 < KV_HEADS:
            score(g + 1)
        mix(g)


def quarter_kernel(place_ref, wd_hbm, out_ref, sem):
    low, core = place_ref[2], place_ref[3]
    width = wd_hbm.shape[1]
    cols = pl.ds(pl.multiple_of((1 - low) * (width // 2) + core * (width // 4), LANES), width // 4)
    copy = pltpu.make_async_copy(wd_hbm.at[:, cols], out_ref, sem)
    copy.start()
    copy.wait()


def near_kernel(split, labels_ref, mask_ref, place_ref, q_hbm, k_hbm, v_hbm, k_ref, v_ref, *rest):
    k_buf, v_buf, bias_buf, s_buf, sem, kv_sem = rest[-6:]
    blocks = len(rest[:-6]) // 4
    outs = [rest[4 * i : 4 * i + 4] for i in range(blocks)]
    tile = outs[0][3].shape[0]
    ctx_here, section = place_ref[0], place_ref[1]
    order = [1 - section, section] if split else list(range(blocks))

    loads = [
        pltpu.make_async_copy(q_hbm.at[pl.ds(pl.multiple_of(t * tile, tile), tile)], outs[i][3], sem.at[i])
        for i, t in enumerate(order)
    ]
    loads.append(pltpu.make_async_copy(k_hbm, k_buf, kv_sem.at[0]))
    loads.append(pltpu.make_async_copy(v_hbm, v_buf, kv_sem.at[1]))
    for copy in loads:
        copy.start()
    for i, t in enumerate(order):
        fill_bias(bias_buf.at[i], mask_ref, labels_ref, ctx_here * blocks + t, [ctx_here, ctx_here ^ 1])
    for copy in loads:
        copy.wait()

    for i, t in enumerate(order):
        sums_ref, totals_ref, limits_ref, q_ref = outs[i]

        @pl.when(labels_ref[0, ctx_here * blocks + t] == section)
        def _():
            def finish(g, sums, totals, limit):
                sums_ref[g] = sums
                totals_ref[g] = totals
                limits_ref[g] = limit

            attend(q_ref, [k_buf, k_ref], [v_buf, v_ref], bias_buf.at[i], s_buf, None, finish)


def attend_far(match, here, pieces, refs, att_ref, bias_buf, s_buf):
    labels_ref, mask_ref, place_ref, key_refs, value_refs, sums_ref, totals_ref, limits_ref, q_ref = refs
    tile, width = att_ref.shape
    group = width // (KV_HEADS * HEAD_DIM)
    opened = fill_bias(bias_buf, mask_ref, labels_ref, here, [place_ref[0] ^ c for c in pieces])

    def finish(g, sums, totals, _):
        attended = (sums / totals).astype(BF16)
        for h in range(group):
            at = (g * group + h) * HEAD_DIM
            att_ref[:, at : at + HEAD_DIM] = attended[h * tile : (h + 1) * tile]

    def prior(g):
        return sums_ref[g], totals_ref[g], limits_ref[g]

    @pl.when(match & (opened > 0))
    def _():
        attend(q_ref, key_refs, value_refs, bias_buf, s_buf, prior, finish)

    @pl.when(match & (opened == 0))
    def _():
        for g in range(KV_HEADS):
            finish(g, sums_ref[g], totals_ref[g], None)


def norm_block(gains_ref, section, first_row, tile, mid_of, norm_buf):
    gain = gains_ref[pl.ds(section, 1), :]
    step = 16

    def norm_rows(j, carry):
        rows = pl.ds(pl.multiple_of(first_row + j * step, step), step)
        mid = mid_of(rows, slice(None))
        factor = lax.rsqrt(jnp.mean(mid * mid, axis=-1, keepdims=True) + 1e-05)
        norm_buf[rows, :] = (mid * factor * gain).astype(BF16)
        return carry

    lax.fori_loop(0, tile // step, norm_rows, 0)


def hidden_of(norm_buf, w_ref, units):
    up_at = w_ref.shape[0] - units
    both = lax.dot_general(norm_buf[...], w_ref[...], OVER_LAST, preferred_element_type=F32)
    gate, upper = both[:, :units], both[:, up_at : up_at + units]
    return (gate * upper / (1.0 + jnp.exp(-gate))).astype(BF16)


def halves_of(place_ref, tile):
    half = tile // 2
    low = place_ref[2]
    own = pl.ds(pl.multiple_of(low * half, half), half)
    return own, pl.ds(pl.multiple_of(half - low * half, half), half)


def far_kernel(split, pieces, labels_ref, mask_ref, place_ref, res_hbm, gains_ref, *rest):
    tile, width = rest[3].shape
    blocks = res_hbm.shape[0] // tile
    state_refs, rest = rest[: 4 * blocks], rest[4 * blocks :]
    count = len(pieces)
    key_refs, value_refs = rest[:count], rest[count : 2 * count]
    wg_hbm, wu_hbm, wd_hbm = rest[2 * count : 2 * count + 3]
    out_refs = rest[2 * count + 3 : -10]
    res_buf, w_buf, wd_buf, bias_buf, s_buf, att_buf, norm_buf, hid_buf, sem, w_sem = rest[-10:]
    if split:
        send_ref, hid_ref, mid_ref, wd_buf, sent_ref = out_refs
    units = wg_hbm.shape[0]
    ctx_here, section, first = place_ref[0], place_ref[1], place_ref[4]
    chosen = [1 - section, section] if split else list(range(blocks))
    refs = (labels_ref, mask_ref, place_ref, key_refs, value_refs)

    loads = []
    for i, t in enumerate(chosen):
        rows = pl.ds(pl.multiple_of(t * tile, tile), tile)
        loads.append(pltpu.make_async_copy(res_hbm.at[rows], res_buf.at[pl.ds(i * tile, tile)], sem.at[i]))
    loads.append(pltpu.make_async_copy(wg_hbm, w_buf.at[pl.ds(0, units)], w_sem.at[0]))
    loads.append(pltpu.make_async_copy(wu_hbm, w_buf.at[pl.ds(w_buf.shape[0] - units, units)], w_sem.at[1]))
    later = pltpu.make_async_copy(wd_hbm, wd_buf, w_sem.at[2])
    for copy in loads:
        copy.start()
    later.start()

    matches = [labels_ref[0, ctx_here * blocks + t] == section for t in chosen]
    for i, t in enumerate(chosen):
        span = pl.ds(i * tile, tile)
        block_refs = (*refs, *state_refs[4 * i : 4 * i + 4])
        attend_far(matches[i], ctx_here * blocks + t, pieces, block_refs, att_buf.at[span], bias_buf, s_buf)

        @pl.when(jnp.logical_not(matches[i]))
        def _():
            norm_buf[span, :] = jnp.zeros((tile, width), BF16)

    for copy in loads:
        copy.wait()

    def mid_of(rows, cols):
        mid = res_buf[rows, cols].astype(F32) + att_buf[rows, cols].astype(F32)
        if split:
            mid_ref[rows, cols] = mid
        return mid

    for i in range(len(chosen)):

        @pl.when(matches[i])
        def _():
            norm_block(gains_ref, section, i * tile, tile, mid_of, norm_buf)

    later.wait()

    @pl.when(functools.reduce(jnp.logical_or, matches))
    def _():
        hid_buf[...] = hidden_of(norm_buf, w_buf, units)
        if split:
            other = halves_of(place_ref, tile)[1]
            other = pl.ds(pl.multiple_of(other.start + tile, other.size), other.size)
            hid_ref[...] = hid_buf[...]
            send_ref[:tile, :] = hid_buf[:tile, :]
            send_ref[tile:, :] = hid_buf[other, :]

            @pl.when(matches[1])
            def _():
                for n in range(0, width // 2, WIDE):
                    cols = pl.ds(pl.multiple_of(place_ref[2] * (width // 2) + n, LANES), WIDE)
                    terms = jnp.dot(hid_buf[other, :], wd_buf[:, cols], preferred_element_type=F32)
                    sent_ref[:, n : n + WIDE] = terms.astype(BF16)

        else:
            for n in range(0, width, WIDE):
                cols = slice(n, n + WIDE)
                terms = jnp.dot(hid_buf[...], wd_buf[:, cols], preferred_element_type=F32)
                for i in range(blocks):
                    span = slice(i * tile, (i + 1) * tile)
                    kept = terms[span] + mid_of(span, cols) * first.astype(F32)
                    out_refs[0][span, cols] = jnp.where(matches[i], kept, 0.0)

    if not split:

        @pl.when(jnp.logical_not(functools.reduce(jnp.logical_or, matches)))
        def _():
            out_refs[0][...] = jnp.zeros(out_refs[0].shape, F32)


def down_own_kernel(labels_ref, place_ref, hid_ref, mid_ref, wd_ref, out_ref):
    tile, half = out_ref.shape
    ctx_here, section, low = place_ref[0], place_ref[1], place_ref[2]

    @pl.when(labels_ref[0, ctx_here * 2 + 1 - section] == section)
    def _():
        for n in range(0, half, WIDE):
            cols = pl.ds(pl.multiple_of(low * half + n, LANES), WIDE)
            terms = jnp.dot(hid_ref[:tile, :], wd_ref[:, cols], preferred_element_type=F32)
            out_ref[:, n : n + WIDE] = terms + mid_ref[:tile, cols]


def down_leave_kernel(labels_ref, place_ref, in_ref, base_ref, here_ref, there_ref, same_ref, other_ref, token_ref):
    tile, quarter = base_ref.shape[0], here_ref.shape[1]
    ctx_here, section, core = place_ref[0], place_ref[1], place_ref[3]
    match = labels_ref[0, ctx_here * 2 + 1 - section] == section
    token_ref[...] = jnp.zeros(token_ref.shape, F32)
    rows = halves_of(place_ref, tile)

    @pl.when(match)
    def _():
        left = jnp.concatenate([in_ref[span, :] for span in rows], axis=0)
        for from_core, ref in ((core, here_ref), (1 - core, there_ref)):
            for n in range(0, quarter, WIDE):
                wide = min(WIDE, quarter - n)
                cols = pl.ds(pl.multiple_of(from_core * quarter + n, LANES), wide)
                terms = jnp.dot(left, ref[:, n : n + wide], preferred_element_type=F32)
                for i, to_ref in enumerate((same_ref, other_ref)):
                    part = terms[i * tile // 2 : (i + 1) * tile // 2] + base_ref[rows[i], cols]
                    to_ref[:, cols] = part.astype(BF16)

    @pl.when(jnp.logical_not(match))
    def _():
        same_ref[...] = jnp.zeros(same_ref.shape, BF16)
        other_ref[...] = jnp.zeros(other_ref.shape, BF16)


def down_stay_kernel(labels_ref, place_ref, in_ref, hid_ref, mid_ref, wd_ref, sum_ref, after_ref, here_ref, there_ref, out_ref):
    tile, quarter = mid_ref.shape[0] // 2, here_ref.shape[1]
    ctx_here, section, low, core = place_ref[0], place_ref[1], place_ref[2], place_ref[3]
    match = labels_ref[0, ctx_here * 2 + section] == section
    own = halves_of(place_ref, tile)[0]
    rows = pl.ds(pl.multiple_of(own.start + tile, own.size), own.size)

    @pl.when(match)
    def _():
        arrived = in_ref[tile:, :]

        def base(cols):
            return jnp.dot(hid_ref[rows, :], wd_ref[:, cols], preferred_element_type=F32) + mid_ref[rows, cols]

        for from_core, ref in ((core, here_ref), (1 - core, there_ref)):
            for n in range(0, quarter, WIDE):
                wide = min(WIDE, quarter - n)
                cols = pl.ds(pl.multiple_of((2 * low + from_core) * quarter + n, LANES), wide)
                terms = jnp.dot(arrived, ref[:, n : n + wide], preferred_element_type=F32)
                out_ref[:, cols] = terms + base(cols)
        for n in range(0, 2 * quarter, WIDE):
            cols = pl.ds(pl.multiple_of((1 - low) * 2 * quarter + n, LANES), WIDE)
            out_ref[:, cols] = sum_ref[:, n : n + WIDE].astype(F32) + base(cols)

    @pl.when(jnp.logical_not(match))
    def _():
        out_ref[...] = jnp.zeros(out_ref.shape, F32)


def last_sum_kernel(place_ref, staying_ref, same_ref, other_ref, out_ref):
    half = same_ref.shape[1]
    low = place_ref[2]
    for at, ref in ((low, same_ref), (1 - low, other_ref)):
        for n in range(0, half, WIDE):
            cols = pl.ds(pl.multiple_of(at * half + n, LANES), WIDE)
            out_ref[:, cols] = (staying_ref[:, cols] + ref[:, n : n + WIDE].astype(F32)).astype(BF16)


SMEM = pl.BlockSpec(memory_space=pltpu.SMEM)
HBM = pl.BlockSpec(memory_space=pltpu.HBM)
VMEM = pl.BlockSpec(memory_space=pltpu.VMEM)
ANY = pl.BlockSpec(memory_space=pl.ANY)


def params(mib):
    return pltpu.CompilerParams(vmem_limit_bytes=mib * 1024 * 1024)


def stay(array):
    return pltpu.with_memory_space_constraint(array, pltpu.HBM)


def cost(flops, moved, powers=0):
    return pl.CostEstimate(flops=flops, bytes_accessed=moved, transcendentals=powers)


def w_down_quarter(place, wd):
    units, width = wd.shape
    return pl.pallas_call(
        quarter_kernel,
        out_shape=jax.ShapeDtypeStruct((units, width // 4), BF16),
        in_specs=[SMEM, HBM],
        out_specs=VMEM,
        scratch_shapes=[pltpu.SemaphoreType.DMA(())],
        compiler_params=params(8),
        cost_estimate=cost(units, units * width),
    )(place, wd)


def near_attention(split, labels, mask, place, queries, own_key, own_value, key, value):
    shard, width = queries.shape
    blocks = shard // BLOCK
    piece_rows, kv_width = key.shape
    rows = width // (KV_HEADS * HEAD_DIM) * BLOCK
    count = 2 * piece_rows
    shape = jax.ShapeDtypeStruct
    state = shape((KV_HEADS, rows, LANES), F32)
    outs = [state, state, state, shape((BLOCK, width), BF16)] * blocks
    made = pl.pallas_call(
        functools.partial(near_kernel, split),
        out_shape=outs,
        in_specs=[SMEM, SMEM, SMEM, HBM, HBM, HBM, VMEM, VMEM],
        out_specs=[VMEM] * len(outs),
        scratch_shapes=[
            pltpu.VMEM((piece_rows, kv_width), BF16),
            pltpu.VMEM((piece_rows, kv_width), BF16),
            pltpu.VMEM((blocks, 2, piece_rows, BLOCK), BF16),
            pltpu.VMEM((2, rows, count), F32),
            pltpu.SemaphoreType.DMA((blocks,)),
            pltpu.SemaphoreType.DMA((2,)),
        ],
        compiler_params=params(16),
        cost_estimate=cost(40 * shard * width * count, 2 * shard * width, shard * width // HEAD_DIM * count),
    )(labels, mask, place, queries, own_key, own_value, key, value)
    return [list(made[4 * i : 4 * i + 4]) for i in range(blocks)]


def far_attention(split, pieces, labels, mask, place, residual, gains, states, keys, values, wg, wu, wd):
    tile, width = states[0][3].shape
    piece_rows = keys[0].shape[0]
    rows = width // (KV_HEADS * HEAD_DIM) * BLOCK
    count = piece_rows * len(pieces)
    units = wg.shape[0]
    up_at = -(-units // LANES) * LANES
    taken = tile * len(states)
    shape = jax.ShapeDtypeStruct
    if split:
        outs = [shape((tile + tile // 2, units), BF16), shape((taken, units), BF16)]
        outs += [shape((taken, width), F32), shape(wd.shape, BF16), shape((tile // 2, width // 2), BF16)]
    else:
        outs = [shape((taken, width), F32)]
    return pl.pallas_call(
        functools.partial(far_kernel, split, pieces),
        out_shape=outs,
        in_specs=[SMEM, SMEM, SMEM, HBM, VMEM] + [VMEM] * (4 * len(states) + 2 * len(pieces)) + [HBM] * 3,
        out_specs=[VMEM] * len(outs),
        scratch_shapes=[
            pltpu.VMEM((taken, width), BF16),
            pltpu.VMEM((up_at + units, width), BF16),
            pltpu.VMEM((16, LANES) if split else wd.shape, BF16),
            pltpu.VMEM((len(pieces), piece_rows, BLOCK), BF16),
            pltpu.VMEM((2, rows, count), F32),
            pltpu.VMEM((taken, width), BF16),
            pltpu.VMEM((taken, width), BF16),
            pltpu.VMEM((taken, units), BF16),
            pltpu.SemaphoreType.DMA((len(states),)),
            pltpu.SemaphoreType.DMA((3,)),
        ],
        compiler_params=params(28),
        cost_estimate=cost(taken * width, width, taken),
    )(
        labels, mask, place, residual, gains, *[array for state in states for array in state],
        *keys, *values, wg, wu, wd,
    )


TOKEN = jax.ShapeDtypeStruct((8, LANES), F32)


def down_own(labels, place, hid, mid, wd):
    rows, width = mid.shape
    return pl.pallas_call(
        down_own_kernel,
        out_shape=jax.ShapeDtypeStruct((rows // 2, width // 2), F32),
        in_specs=[SMEM, SMEM] + [VMEM] * 3,
        out_specs=VMEM,
        compiler_params=params(16),
        cost_estimate=cost(40 * rows * wd.size, wd.size),
    )(labels, place, hid, mid, wd)


def down_leave(labels, place, arrived, base, here, there):
    tile, half_width = base.shape
    half = jax.ShapeDtypeStruct((tile // 2, half_width), BF16)
    return pl.pallas_call(
        down_leave_kernel,
        out_shape=[half, half, TOKEN],
        in_specs=[SMEM, SMEM] + [VMEM] * 4,
        out_specs=[VMEM] * 3,
        compiler_params=params(16),
        cost_estimate=cost(tile, tile),
    )(labels, place, arrived, base, here, there)


def down_stay(labels, place, arrived, hid, mid, wd, summed, after, here, there):
    rows, width = mid.shape
    return pl.pallas_call(
        down_stay_kernel,
        out_shape=jax.ShapeDtypeStruct((rows // 4, width), F32),
        in_specs=[SMEM, SMEM] + [VMEM] * 5 + [ANY] + [VMEM] * 2,
        out_specs=VMEM,
        compiler_params=params(16),
        cost_estimate=cost(40 * rows * wd.size, wd.size),
    )(labels, place, arrived, hid, mid, wd, summed, after, here, there)


def last_sum(place, staying, same, other):
    return pl.pallas_call(
        last_sum_kernel,
        out_shape=jax.ShapeDtypeStruct(staying.shape, BF16),
        in_specs=[SMEM] + [VMEM] * 3,
        out_specs=VMEM,
        compiler_params=params(8),
        cost_estimate=cost(staying.size, staying.size),
    )(place, staying, same, other)


def xor_pairs(count, bits):
    return [(i, i ^ bits) for i in range(count)]


def per_device(queries, keys, values, residual, labels, block_mask, gains, w_gate, w_up, w_down):
    shard, width = queries.shape[1:]
    exp_count = lax.axis_size("exp")
    exp_here = lax.axis_index("exp")
    ctx_count = lax.axis_size("ctx")
    ctx_here = lax.axis_index("ctx")
    half = exp_count // 2
    split = exp_count == 4 and shard == 2 * BLOCK and ctx_count == 4
    section = exp_here // half
    low = exp_here % 2 if split else jnp.zeros_like(exp_here)
    core = ctx_here % 2
    first = exp_here % half == 0
    place = jnp.stack([value.astype(jnp.int32) for value in (ctx_here, section, low, core, first)])
    labels, block_mask, gains = stay(labels), stay(block_mask), stay(gains)
    own_q, own_res = stay(queries[0]), stay(residual[0])

    held = {0: (keys[0], values[0])}

    def spread(bits):
        pairs = xor_pairs(ctx_count, bits)
        for at, (k, v) in list(held.items()):
            held[at ^ bits] = (lax.ppermute(k, "ctx", pairs), lax.ppermute(v, "ctx", pairs))

    def swap(array):
        return lax.ppermute(array, "ctx", xor_pairs(ctx_count, 1))

    bits = ctx_count // 2
    while bits > 1:
        spread(bits)
        bits //= 2
    held[1] = (swap(keys[0]), swap(values[0]))
    z_pairs = xor_pairs(exp_count, 1)
    if split:
        here = lax.ppermute(w_down_quarter(place, stay(w_down)), "exp", z_pairs)
    states = near_attention(
        split, labels, block_mask, place, own_q, stay(keys[0]), stay(values[0]), *held[1]
    )
    for at in range(2, ctx_count, 2):
        k, v = held[at]
        k, states[0][0] = lax.optimization_barrier((k, states[0][0]))
        v, states[0][1] = lax.optimization_barrier((v, states[0][1]))
        held[at] = (k, v)
        held[at + 1] = (swap(k), swap(v))
    far = range(2, ctx_count)
    far_keys, far_values = [held[c][0] for c in far], [held[c][1] for c in far]
    weights = (far_keys, far_values, stay(w_gate.T), stay(w_up.T), stay(w_down))
    shared = (labels, block_mask, place, own_res, gains)
    made = far_attention(split, far, *shared, states, *weights)
    if not split:
        return lax.psum_scatter(made[0][None], "exp", scatter_dimension=1, tiled=True).astype(BF16)

    send, hid, mid, own_wd, sent = made
    here, send = lax.optimization_barrier((here, send))
    there = swap(here)
    arrived = lax.ppermute(send, "exp", z_pairs)
    base = down_own(labels, place, hid, mid, own_wd)
    sent, there = lax.optimization_barrier((sent, there))
    same, other, token = down_leave(labels, place, arrived, base, here, there)
    same, other = (
        lax.ppermute(part, "exp", xor_pairs(exp_count, bits)) for part, bits in ((same, 2), (other, 3))
    )
    summed = lax.ppermute(sent, "exp", z_pairs)
    staying = down_stay(labels, place, arrived, hid, mid, own_wd, summed, token, here, there)
    return last_sum(place, staying, same, other)[None]


def solution(mesh):
    placed = (
        P("dp", "ctx", None),
        P("dp", "ctx", None),
        P("dp", "ctx", None),
        P("dp", "ctx", None),
        P("dp", None),
        P("dp", None, None),
        P(),
        P(None, "exp"),
        P(None, "exp"),
        P("exp", None),
    )
    return jax.shard_map(
        per_device,
        mesh=mesh,
        in_specs=placed,
        out_specs=P("dp", ("ctx", "exp"), None),
        check_vma=False,
    )
```
